256 devices in a mesh: ctx: 32 (over z, x), tp: 8 (over y, core).
Axes of the slice: x: 4, y: 4, z: 8, core: 2. Of those that a mesh axis runs over, the one named last changes fastest.
Arguments:
- streams: bfloat16 [4096, 3, 8192], P('ctx', None, 'tp'), may hold values from -6 to 6
- short_filter: float32 [7, 3, 8192], P(None, None, 'tp'), may hold values from -2 to 2
- long_filter: float32 [128, 8192], P(None, 'tp'), may hold values from -1 to 1
- hyena_grad: bfloat16 [4096, 8192], P('ctx', 'tp'), may hold values from -8 to 8
- queries: bfloat16 [4096, 4096], P('ctx', 'tp'), may hold values from -4000 to 4000
- keys: bfloat16 [4096, 4096], P('ctx', 'tp'), may hold values from -4000 to 4000
- values: bfloat16 [4096, 4096], P('ctx', 'tp'), may hold values from -6 to 6
- gain_q: float32 [4096], P('tp'), may hold values from 0.5 to 1.5
- gain_k: float32 [4096], P('tp'), may hold values from 0.5 to 1.5
- attn_grad: bfloat16 [4096, 4096], P('ctx', 'tp'), may hold values from -8 to 8
Outputs:
- hyena_out: bfloat16 [4096, 8192], P('ctx', 'tp')
- grad_streams: bfloat16 [4096, 3, 8192], P('ctx', None, 'tp')
- grad_short: float32 [7, 3, 8192], P(None, None, 'tp')
- grad_long: float32 [128, 8192], P(None, 'tp')
- attn_out: bfloat16 [4096, 4096], P('ctx', 'tp')
- grad_q: bfloat16 [4096, 4096], P('ctx', 'tp')
- grad_k: bfloat16 [4096, 4096], P('ctx', 'tp')
- grad_v: bfloat16 [4096, 4096], P('ctx', 'tp')
- grad_gain_q: float32 [4096], P('tp')
- grad_gain_k: float32 [4096], P('tp')
The draws below stay inside these ranges and needn't reach their ends.
All inputs are finite; a program needn't handle non-finite values.
Results may differ from the reference program's by a relative error of at most 0.035.
Values may be sent and summed in bfloat16 or wider, within the bound.
No kernel may reach another device: no remote copies, remote signals or barrier semaphores. Data moves between devices by JAX's collectives and lax.ppermute only.
A program may use at most 128 MiB of HBM per device.

```python
import math
import jax
import jax.numpy as jnp
from jax import lax

D = 8192
HEADS = 32
HD = 128
STAPS = 7
LTAPS = 128
SEQ = 4096
WIDTH = 4096


def clipped_normal(key, shape):
    return jnp.clip(jax.random.normal(key, shape, jnp.float32), -4.0, 4.0)


def column_rise(count):
    return 3.0 ** (jnp.arange(count, dtype=jnp.float32) / count)


def drawn_rows():
    positions = jnp.arange(SEQ, dtype=jnp.int32)
    return (positions % 64 == 0) & (positions > 0)


def head_strength(key, lift):
    spread = jnp.exp(2.0 * jax.random.uniform(jax.random.fold_in(key, 201), (SEQ, HEADS, 1), jnp.float32))
    boost = 10.0 + 20.0 * jax.random.uniform(jax.random.fold_in(key, 202), (SEQ, 1, 1), jnp.float32)
    chosen_head = jnp.arange(SEQ, dtype=jnp.int32) // 64 % HEADS
    chosen = jnp.arange(HEADS, dtype=jnp.int32)[None, :, None] == chosen_head[:, None, None]
    extra = jnp.where(chosen & drawn_rows()[:, None, None], boost, 1.0)
    return (spread * extra) ** lift


def shared_keys(key, lift):
    base = clipped_normal(jax.random.fold_in(key, 101), (SEQ, HEADS, HD))
    scaled = base * head_strength(key, lift)
    before = jnp.roll(drawn_rows(), -1)[:, None, None]
    mixed_rows = jnp.where(before, scaled, scaled)
    return mixed_rows.reshape(SEQ, HEADS * HD) * column_rise(HEADS * HD)


def draw_keys(key, part):
    lift = 0.0
    return shared_keys(key, lift).astype(jnp.bfloat16)


def draw_queries(key, part):
    lift = 0.0
    matched = shared_keys(key, lift)
    key = jax.random.fold_in(key, 5)
    own_rows = clipped_normal(key, (SEQ, HEADS, HD)) * head_strength(key, lift)
    own_rows = own_rows.reshape(SEQ, HEADS * HD) * column_rise(HEADS * HD)
    take = drawn_rows()[:, None] & (lift > 0.5)
    return jnp.where(take, matched, own_rows).astype(jnp.bfloat16)


def draw_long_filter(key, part):
    key = jax.random.fold_in(key, 7)
    low_rate = 1.0 / 600.0
    high_rate = 1.0 / 20.0
    noise = clipped_normal(jax.random.fold_in(key, 1), (LTAPS, D))
    exponent = jax.random.uniform(jax.random.fold_in(key, 2), (1, D), jnp.float32, jnp.log(low_rate), jnp.log(high_rate))
    taps = jnp.arange(LTAPS, dtype=jnp.float32)[:, None]
    return 0.25 * noise * jnp.exp(-taps * jnp.exp(exponent))


def draw_hyena_grad(key, part):
    key = jax.random.fold_in(key, 11)
    rise = (3.0 ** (jnp.arange(SEQ, dtype=jnp.float32) / SEQ))[:, None]
    noise = clipped_normal(key, (SEQ, D))
    return (0.5 * noise * rise).astype(jnp.bfloat16)


def draw_attn_grad(key, part):
    key = jax.random.fold_in(key, 13)
    rise = (3.0 ** (jnp.arange(SEQ, dtype=jnp.float32) / SEQ))[:, None]
    noise = clipped_normal(key, (SEQ, HEADS * HD))
    return (0.5 * noise * rise).astype(jnp.bfloat16)


def shard_levels(stream_key, extent, split, smallest, top_value):
    level, own = 1.0, jax.random.fold_in(stream_key, 6)
    for axis_at, parts in split:
        heights = jnp.exp(jax.random.uniform(jax.random.fold_in(own, axis_at), (parts,), jnp.float32, smallest / len(split), top_value / len(split)))
        level = level * jnp.repeat(heights, extent[axis_at] // parts).reshape([-1 if axis == axis_at else 1 for axis in range(len(extent))])
    return level


def centred(rng, dims, scale, reach, shards=(), held_as=jnp.bfloat16):
    loudness = shard_levels(rng, dims, shards, -0.22, 0.18) if shards else 1.0
    entries = jax.random.normal(rng, dims, jnp.float32) * scale * loudness
    return jnp.minimum(jnp.maximum(entries, -reach), reach).astype(held_as)


def setup_inputs(seed: int = 0) -> dict:
    splits = jax.random.split(jax.random.key(seed), 11)
    return {
        "streams": centred(splits[0], (SEQ, 3, D), 1.0, 6.0, ((0, 32), (2, 8))),
        "short_filter": centred(splits[1], (STAPS, 3, D), STAPS ** -0.5, 2.0, ((2, 8),), jnp.float32),
        "long_filter": draw_long_filter(jax.random.fold_in(splits[10], 71), 0),
        "hyena_grad": draw_hyena_grad(jax.random.fold_in(splits[10], 71), 0),
        "queries": draw_queries(jax.random.fold_in(splits[10], 71), 0),
        "keys": draw_keys(jax.random.fold_in(splits[10], 71), 0),
        "values": centred(splits[6], (SEQ, WIDTH), 1.0, 6.0, ((0, 32), (1, 8))),
        "gain_q": jnp.clip(1.0 + 0.1 * jax.random.normal(splits[7], (WIDTH,), jnp.float32), 0.5, 1.5),
        "gain_k": jnp.clip(1.0 + 0.1 * jax.random.normal(splits[8], (WIDTH,), jnp.float32), 0.5, 1.5),
        "attn_grad": draw_attn_grad(jax.random.fold_in(splits[10], 71), 0),
    }


EPS = 1e-06
MASKED = -1e+30

def causal_taps(values_in, filter_taps):
    tap_count = filter_taps.shape[0]
    length = values_in.shape[0]
    padding = jnp.zeros((tap_count - 1,) + values_in.shape[1:], values_in.dtype)
    padded = jnp.concatenate([padding, values_in], 0)

    def step(running, tap_idx):
        window = lax.dynamic_slice_in_dim(padded, (tap_count - 1 - tap_idx).astype(jnp.int32), length, 0)
        return (running + filter_taps[tap_idx] * window, None)
    running, _ = lax.scan(step, jnp.zeros_like(values_in), jnp.arange(tap_count, dtype=jnp.int32))
    return running

def later_taps(values_in, filter_taps):
    tap_count = filter_taps.shape[0]
    length = values_in.shape[0]
    padding = jnp.zeros((tap_count - 1,) + values_in.shape[1:], values_in.dtype)
    padded = jnp.concatenate([values_in, padding], 0)

    def step(running, tap_idx):
        window = lax.dynamic_slice_in_dim(padded, tap_idx.astype(jnp.int32), length, 0)
        return (running + filter_taps[tap_idx] * window, None)
    running, _ = lax.scan(step, jnp.zeros_like(values_in), jnp.arange(tap_count, dtype=jnp.int32))
    return running

def tap_grads(later_vals, values_in, tap_count):
    length = values_in.shape[0]
    padding = jnp.zeros((tap_count - 1,) + values_in.shape[1:], values_in.dtype)
    padded = jnp.concatenate([padding, values_in], 0)

    def one_tap(tap_idx):
        window = lax.dynamic_slice_in_dim(padded, (tap_count - 1 - tap_idx).astype(jnp.int32), length, 0)
        return lax.optimization_barrier(jnp.sum(later_vals * window, 0))
    return lax.map(one_tap, jnp.arange(tap_count, dtype=jnp.int32))

def normed(raw, gain):
    wide = raw.astype(jnp.float32)
    rate = lax.rsqrt(lax.optimization_barrier(jnp.mean(wide * wide, axis=1, keepdims=True)) + EPS)
    return ((wide * rate * gain).astype(jnp.bfloat16), wide, rate)

def norm_back(wide, rate, gain, grad_normed):
    scaled = grad_normed * gain
    inner_sum = lax.optimization_barrier(jnp.sum(scaled * wide, axis=1, keepdims=True))
    full_width = wide.shape[1]
    grad_raw = (rate * scaled - wide * rate * rate * rate * inner_sum / full_width).astype(jnp.bfloat16)
    grad_gain = lax.optimization_barrier(jnp.sum(grad_normed * wide * rate, 0))
    return (grad_raw, grad_gain)

def reference(streams, short_filter, long_filter, hyena_grad, queries, keys, values, gain_q, gain_k, attn_grad):
    inputs = streams.astype(jnp.float32)
    short_mixed = causal_taps(inputs, short_filter)
    product = lax.optimization_barrier((short_mixed[:, 1] * short_mixed[:, 2]).astype(jnp.bfloat16))
    product_wide = product.astype(jnp.float32)
    filtered = causal_taps(product_wide, long_filter)
    hyena_out = (short_mixed[:, 0] * filtered).astype(jnp.bfloat16)
    upstream = hyena_grad.astype(jnp.float32)
    grad_filtered = upstream * short_mixed[:, 0]
    grad_gate = upstream * filtered
    grad_product = later_taps(grad_filtered, long_filter)
    grad_long = tap_grads(grad_filtered, product_wide, long_filter.shape[0])
    grad_mixed = jnp.stack([grad_gate, grad_product * short_mixed[:, 2], grad_product * short_mixed[:, 1]], 1)
    grad_streams = later_taps(grad_mixed, short_filter).astype(jnp.bfloat16)
    grad_short = tap_grads(grad_mixed, inputs, short_filter.shape[0])
    normed_q, wide_q, rate_q = normed(queries, gain_q)
    normed_k, wide_k, rate_k = normed(keys, gain_k)
    length = queries.shape[0]
    scale = 1.0 / math.sqrt(HD)
    positions = jnp.arange(length, dtype=jnp.int32)
    allowed = positions[None, :] <= positions[:, None]

    def split_heads(matrix):
        return matrix.reshape(length, HEADS, HD).transpose(1, 0, 2)

    def merge_heads(stacked):
        return stacked.transpose(1, 0, 2).reshape(length, HEADS * HD)

    def one_head(items):
        query_head, key_head, value_head, grad_head = items
        scores = jnp.dot(query_head, key_head.T, preferred_element_type=jnp.float32) * scale
        scores = jnp.where(allowed, scores, MASKED)
        row_max = lax.optimization_barrier(jnp.max(scores, axis=1, keepdims=True))
        log_total = row_max + jnp.log(lax.optimization_barrier(jnp.sum(jnp.exp(scores - row_max), axis=1, keepdims=True)))
        weights = jnp.where(allowed, jnp.exp(scores - log_total), 0.0).astype(jnp.bfloat16)
        head_out = jnp.dot(weights, value_head, preferred_element_type=jnp.float32).astype(jnp.bfloat16)
        head_out = lax.optimization_barrier(head_out)
        row_spread = lax.optimization_barrier(jnp.sum(grad_head.astype(jnp.float32) * head_out.astype(jnp.float32), axis=1, keepdims=True))
        grad_dots = jnp.dot(grad_head, value_head.T, preferred_element_type=jnp.float32)
        slopes = (weights.astype(jnp.float32) * (grad_dots - row_spread)).astype(jnp.bfloat16)
        grad_value = jnp.dot(weights.T, grad_head, preferred_element_type=jnp.float32)
        grad_query = jnp.dot(slopes, key_head, preferred_element_type=jnp.float32) * scale
        grad_key = jnp.dot(slopes.T, query_head, preferred_element_type=jnp.float32) * scale
        return (head_out, grad_query, grad_key, grad_value)
    head_outs, grad_nq, grad_nk, grad_values = lax.map(one_head, (split_heads(normed_q), split_heads(normed_k), split_heads(values), split_heads(attn_grad)))
    attn_out = merge_heads(head_outs)
    grad_v = merge_heads(grad_values).astype(jnp.bfloat16)
    grad_q, grad_gain_q = norm_back(wide_q, rate_q, gain_q, merge_heads(grad_nq))
    grad_k, grad_gain_k = norm_back(wide_k, rate_k, gain_k, merge_heads(grad_nk))
    return (hyena_out, grad_streams, grad_short, grad_long, attn_out, grad_q, grad_k, grad_v, grad_gain_q, grad_gain_k)
```

```python
import functools
import math

import jax
import jax.numpy as jnp
import numpy as np
from jax import lax
from jax.experimental import pallas as pl
from jax.experimental.pallas import tpu as pltpu
from jax.sharding import Mesh
from jax.sharding import PartitionSpec as P

HD = 128
EPS = 1e-06
MASKED = -1e30
ROWS = 128
NZ, NX, NY, NC = 8, 4, 4, 2
HALF = 64
F32 = jnp.float32
BF16 = jnp.bfloat16
VMEM_LIMIT = 48 * 1024 * 1024


def call(kernel, outs, scratch=(), flops=0, moved=0, exps=0, **kw):
    return pl.pallas_call(
        kernel,
        out_shape=outs,
        scratch_shapes=list(scratch),
        compiler_params=pltpu.CompilerParams(vmem_limit_bytes=VMEM_LIMIT),
        cost_estimate=pl.CostEstimate(flops=flops, bytes_accessed=moved, transcendentals=exps),
        **kw,
    )


def shape(dims, dtype):
    return jax.ShapeDtypeStruct(dims, dtype)


VM = pl.BlockSpec(memory_space=pltpu.VMEM)
SM = pl.BlockSpec(memory_space=pltpu.SMEM)


def transform_tables():
    n = np.arange(256)
    k = np.arange(128) + 0.5
    angle = 2.0 * np.pi * np.outer(k, n) / 256.0
    fwd = np.concatenate([np.cos(angle), -np.sin(angle)], 0)
    inv = np.concatenate([np.cos(angle), -np.sin(angle)], 0).T / 128.0
    lag = inv[128 - np.arange(128)]
    tables = [fwd[:, :128], fwd[:, 128:], inv[128:], inv[:128], lag]
    parts = []
    for t in tables:
        t32 = t.astype(np.float32)
        hi = t32.astype(jnp.bfloat16)
        lo = (t32 - hi.astype(np.float32)).astype(jnp.bfloat16)
        parts.append(np.stack([hi, lo]))
    return parts


def mm(a, b):
    return jnp.dot(a, b, preferred_element_type=F32)


def table_dot(table, x):
    hi, lo = table[0], table[1]
    if x.dtype == BF16:
        return mm(hi, x) + mm(lo, x)
    xh = x.astype(BF16)
    xl = (x - xh.astype(F32)).astype(BF16)
    return mm(hi, xh) + mm(lo, xh) + mm(hi, xl)


def short_kernel(st, rim, sf, hg, sm, prod, gf, ext):
    for s in range(3):
        ext[s, 0:16] = rim[s].astype(F32)
        ext[s, 16:144] = st[s].astype(F32)
        total = None
        for j in range(7):
            term = sf[j, s : s + 1, :] * ext[s, 16 - j : 144 - j, :]
            total = term if total is None else total + term
        sm[s] = total
    prod[...] = (sm[1] * sm[2]).astype(BF16)
    gf[...] = (hg[...].astype(F32) * sm[0]).astype(BF16)


def long_kernel(
    sm, hg, prod, prod_prev, gf_next, st, rim, sf, lf, fa, fb, iv_f, iv_g, iv_l,
    out, gs, head, tail, red, ext, gm,
):
    gate, one, two = sm[0], sm[1], sm[2]
    up = hg[...].astype(F32)
    gf = up * gate
    spec_x = table_dot(fa, prod_prev[...]) + table_dot(fb, prod[...])
    spec_h = table_dot(fa, lf[...])
    spec_g0 = table_dot(fa, gf)
    spec_g = spec_g0 + table_dot(fb, gf_next[...])
    xr, xi = spec_x[:128], spec_x[128:]
    hr, hi = spec_h[:128], spec_h[128:]
    filt = table_dot(iv_f, jnp.concatenate([xr * hr - xi * hi, xr * hi + xi * hr], 0))
    out[...] = (gate * filt).astype(BF16)
    gr, gi = spec_g[:128], spec_g[128:]
    gprod = table_dot(iv_g, jnp.concatenate([gr * hr + gi * hi, gi * hr - gr * hi], 0))
    ar, ai = spec_g0[:128], spec_g0[128:]
    glong = table_dot(iv_l, jnp.concatenate([ar * xr + ai * xi, ar * xi - ai * xr], 0))
    red[0:128] = glong.astype(BF16)
    gm[:, 128:144] = jnp.zeros_like(gm[:, 128:144])
    gm[0, 0:128] = up * filt
    gm[1, 0:128] = gprod * two
    gm[2, 0:128] = gprod * one
    rows = []
    for s in range(3):
        head[s] = gm[s, 0:16].astype(BF16)
        ext[0:16] = rim[s].astype(F32)
        ext[16:144] = st[s].astype(F32)
        own = gm[s, 0:128]
        total = None
        for j in range(7):
            term = sf[j, s : s + 1, :] * gm[s, j : j + 128, :]
            total = term if total is None else total + term
            rows.append(jnp.sum(own * ext[16 - j : 144 - j, :], axis=0, keepdims=True))
        rows.append(jnp.zeros_like(rows[-1]))
        gs[s] = total.astype(BF16)
        tail[s] = total[112:128]
    rows.append(jnp.zeros((40, rows[-1].shape[1]), F32))
    red[128:192] = jnp.concatenate(rows, 0).astype(BF16)


def to_lanes(col_q, col_k):
    both = jnp.concatenate([col_q, col_k], 0)
    return jnp.transpose(jnp.broadcast_to(both, (128, 128)))[0:8]


def to_columns(lanes):
    wide = jnp.transpose(jnp.broadcast_to(lanes[0:1], (128, 128)))
    return wide[0:64, 0:1], wide[64:128, 0:1]


def lane_sum(x):
    total = x[:, 0:128]
    for h in range(1, x.shape[1] // 128):
        total = total + x[:, h * 128 : (h + 1) * 128]
    return jnp.sum(total, axis=1, keepdims=True)


def own_rows(ref, core):
    return ref[pl.ds(pl.multiple_of(core * HALF, HALF), HALF), :]


def square_kernel(idx, keys, queries, other, out):
    core = idx[1]
    sums = []
    for ref, slot in ((queries, 2), (keys, 0)):
        a = own_rows(ref, core).astype(F32)
        b = other[slot].astype(F32)
        sums.append(lane_sum(a * a + b * b))
    out[...] = to_lanes(sums[0], sums[1])


def pack_kernel(idx, keys, values, queries, grads, other, g_own, g_other, s0, s1, s2, s3, out, rates):
    core = idx[1]
    rate = lax.rsqrt((s0[...] + s1[...] + s2[...] + s3[...]) / (NY * 8 * HD) + EPS)
    rates[...] = rate
    rate_q, rate_k = to_columns(rate)
    rows = [own_rows(r, core) for r in (keys, values, queries, grads)]
    for h in range(4):
        cols = slice(h * 128, (h + 1) * 128)
        for mine in (True, False):
            slot = core * 4 + h if mine else (1 - core) * 4 + h
            gains = g_own if mine else g_other
            parts = [rows[a][:, cols] if mine else other[a][:, cols] for a in range(4)]
            out[slot, 0:64] = (parts[0].astype(F32) * rate_k * gains[1:2, cols]).astype(BF16)
            out[slot, 64:128] = parts[1]
            out[slot, 128:192] = (parts[2].astype(F32) * rate_q * gains[0:1, cols]).astype(BF16)
            out[slot, 192:256] = parts[3]


def attention_kernel(
    idx, blk, m0, m1, m2, m3, o0, o1, o2, o3,
    keep, gkeep, csend, osend,
    k_all, v_all, q_all, d_all, s_all, w_all,
):
    my_x, core = idx[0], idx[1]
    for d, refs in enumerate(((m0, o0), (m1, o1), (m2, o2), (m3, o3))):
        xd = lax.rem(my_x + NX - d, NX)
        for ref, cc in zip(refs, (core, 1 - core)):
            at = pl.multiple_of(xd * 128 + cc * 64, 64)
            for z in range(NZ):
                k_all[z, pl.ds(at, 64)] = ref[z * 128 : z * 128 + 64]
                v_all[z, pl.ds(at, 64)] = ref[z * 128 + 64 : z * 128 + 128]
    for z in range(NZ):
        q_all[z * 64 : z * 64 + 64] = blk[z, 128:192]
        d_all[z * 64 : z * 64 + 64] = blk[z, 192:256]
    scale = 1.0 / math.sqrt(HD)
    power = scale * math.log2(math.e)
    base = my_x * 128 + core * 64
    nt = (((1,), (1,)), ((), ()))
    tn = (((0,), (0,)), ((), ()))

    def first(kz):
        return (kz // 2) * 128

    key_row = lax.broadcasted_iota(jnp.int32, (512, 128), 0)
    lane = lax.broadcasted_iota(jnp.int32, (512, 128), 1)
    query_row = (lane // 64) * 512 + base + lane % 64

    row_max = jnp.full((1, 512), MASKED, F32)
    for kz in range(NZ):
        lo = first(kz)
        sc = lax.dot_general(k_all[kz], q_all[lo:512], nt, preferred_element_type=F32)
        diag = jnp.where(key_row + (kz % 2) * 512 <= query_row, sc[:, 0:128], MASKED)
        sc = diag if lo == 384 else jnp.concatenate([diag, sc[:, 128:]], 1)
        s_all[kz, :, lo:512] = sc
        top = jnp.max(sc, axis=0, keepdims=True)
        top = jnp.maximum(row_max[:, lo:], top)
        row_max = top if lo == 0 else jnp.concatenate([row_max[:, :lo], top], 1)
    row_sum = jnp.zeros((1, 512), F32)
    for kz in range(NZ):
        lo = first(kz)
        p = jnp.exp2((s_all[kz, :, lo:512] - row_max[:, lo:]) * power)
        s_all[kz, :, lo:512] = p
        more = row_sum[:, lo:] + jnp.sum(p, axis=0, keepdims=True)
        row_sum = more if lo == 0 else jnp.concatenate([row_sum[:, :lo], more], 1)
    inv = 1.0 / row_sum
    out_t = jnp.zeros((128, 512), F32)
    for kz in range(NZ):
        lo = first(kz)
        w = (s_all[kz, :, lo:512] * inv[:, lo:]).astype(BF16)
        w_all[kz, :, lo:512] = w
        piece = out_t[:, lo:] + lax.dot_general(v_all[kz], w, tn, preferred_element_type=F32)
        out_t = piece if lo == 0 else jnp.concatenate([out_t[:, :lo], piece], 1)
    out_b = jnp.transpose(out_t).astype(BF16)
    spread_col = jnp.sum(out_b.astype(F32) * d_all[...].astype(F32), axis=1, keepdims=True)
    spread = jnp.transpose(jnp.broadcast_to(spread_col, (512, 128)))[0:1]
    grad_qt = jnp.zeros((128, 512), F32)
    gain_k = jnp.zeros((1, 128), F32)
    for kz in range(NZ):
        lo = first(kz)
        w = w_all[kz, :, lo:512]
        dp = lax.dot_general(v_all[kz], d_all[lo:512], nt, preferred_element_type=F32)
        ds = (w.astype(F32) * (dp - spread[:, lo:])).astype(BF16)
        grad_v = mm(w, d_all[lo:512])
        grad_k = mm(ds, q_all[lo:512]) * scale
        piece = grad_qt[:, lo:] + lax.dot_general(k_all[kz], ds, tn, preferred_element_type=F32)
        grad_qt = piece if lo == 0 else jnp.concatenate([grad_qt[:, :lo], piece], 1)
        gain_k = gain_k + jnp.sum(grad_k * k_all[kz].astype(F32), axis=0, keepdims=True)
        for xx in range(NX):
            at = xx * 1024 + kz * 128
            for arr, val in enumerate((grad_k, grad_v)):
                dst = slice(at + arr * 64, at + arr * 64 + 64)
                half0 = val[xx * 128 : xx * 128 + 64]
                half1 = val[xx * 128 + 64 : xx * 128 + 128]
                keep[dst] = jnp.where(core == 0, half0, half1)
                csend[dst] = jnp.where(core == 0, half1, half0).astype(BF16)
    grad_q = jnp.transpose(grad_qt) * scale
    gain_q = jnp.sum(grad_q * q_all[...].astype(F32), axis=0, keepdims=True)
    gains = jnp.concatenate([gain_q, gain_k, jnp.zeros((6, 128), F32)], 0)
    gkeep[...] = gains
    high = gains.astype(BF16).astype(F32)
    csend[4096:4112] = jnp.concatenate([high, gains - high], 0).astype(BF16)
    for z in range(NZ):
        osend[z, 0:64] = out_b[z * 64 : z * 64 + 64]
        osend[z, 64:128] = grad_q[z * 64 : z * 64 + 64].astype(BF16)


def gains_of(rows16):
    wide = rows16.astype(F32)
    return wide[0:8] + wide[8:16]


def core_sum_kernel(idx, keep, gkeep, other, s0, g0, s1, s2, s3):
    my_x = idx[0]
    gains = gkeep[...] + gains_of(other[4096:4112])
    g0[...] = gains
    high = gains.astype(BF16).astype(F32)
    rows = jnp.concatenate([high, gains - high], 0).astype(BF16)
    for d, ref in enumerate((s0, s1, s2, s3)):
        at = pl.multiple_of(lax.rem(my_x + d, NX) * 1024, 1024)
        total = keep[pl.ds(at, 1024)] + other[pl.ds(at, 1024)].astype(F32)
        ref[0:1024] = total.astype(ref.dtype)
        if d:
            ref[1024:1040] = rows


def ring_sum_kernel(s0, g0, r1, r2, r3, osend, out):
    gains = g0[...] + gains_of(r1[1024:1040]) + gains_of(r2[1024:1040]) + gains_of(r3[1024:1040])
    high = gains.astype(BF16).astype(F32)
    rows = jnp.concatenate([high, gains - high], 0).astype(BF16)
    for z in range(NZ):
        at = slice(z * 128, z * 128 + 128)
        total = s0[at] + r1[at].astype(F32) + r2[at].astype(F32) + r3[at].astype(F32)
        out[z, 0:128] = total.astype(BF16)
        out[z, 128:256] = osend[z]
        out[z, 256:272] = rows


def inner_kernel(idx, back, keys, queries, other, g_own, g_other, part, gains, mine, send):
    core = idx[1]
    own_k, own_q = own_rows(keys, core), own_rows(queries, core)
    sum_q = jnp.zeros((64, 128), F32)
    sum_k = jnp.zeros((64, 128), F32)
    for h in range(4):
        cols = slice(h * 128, (h + 1) * 128)
        for is_own in (True, False):
            slot = core * 4 + h if is_own else (1 - core) * 4 + h
            gain = g_own if is_own else g_other
            raw_k = own_k[:, cols] if is_own else other[0][:, cols]
            raw_q = own_q[:, cols] if is_own else other[2][:, cols]
            gk = back[slot, 0:64].astype(F32)
            gq = back[slot, 192:256].astype(F32)
            sum_q = sum_q + gq * gain[0:1, cols] * raw_q.astype(F32)
            sum_k = sum_k + gk * gain[1:2, cols] * raw_k.astype(F32)
            dst = mine if is_own else send
            dst[0, :, cols] = back[slot, 64:128]
            dst[1, :, cols] = back[slot, 128:192]
        got = gains_of(back[core * 4 + h, 256:272])
        gains[0:1, cols] = got[0:1] / g_own[0:1, cols]
        gains[1:2, cols] = got[1:2] / g_own[1:2, cols]
    part[...] = to_lanes(
        jnp.sum(sum_q, axis=1, keepdims=True), jnp.sum(sum_k, axis=1, keepdims=True)
    )


def norm_kernel(idx, back, keys, queries, other, g_own, g_other, rates, p0, p1, p2, p3, mine, send):
    core = idx[1]
    rate_q, rate_k = to_columns(rates[...])
    inner_q, inner_k = to_columns(p0[...] + p1[...] + p2[...] + p3[...])
    width = NY * 8 * HD
    coef_q = rate_q * rate_q * rate_q * inner_q / width
    coef_k = rate_k * rate_k * rate_k * inner_k / width
    own_k, own_q = own_rows(keys, core), own_rows(queries, core)
    for h in range(4):
        cols = slice(h * 128, (h + 1) * 128)
        for is_own in (True, False):
            slot = core * 4 + h if is_own else (1 - core) * 4 + h
            gain = g_own if is_own else g_other
            raw_k = own_k[:, cols] if is_own else other[0][:, cols]
            raw_q = own_q[:, cols] if is_own else other[2][:, cols]
            gk = back[slot, 0:64].astype(F32)
            gq = back[slot, 192:256].astype(F32)
            dst = mine if is_own else send
            dst[0, :, cols] = (
                rate_q * (gq * gain[0:1, cols]) - raw_q.astype(F32) * coef_q
            ).astype(BF16)
            dst[1, :, cols] = (
                rate_k * (gk * gain[1:2, cols]) - raw_k.astype(F32) * coef_k
            ).astype(BF16)


def join_kernel(idx, mine, got, mine_qk, got_qk, v_out, o_out, q_out, k_out):
    core = idx[1]
    here = pl.ds(pl.multiple_of(core * HALF, HALF), HALF)
    there = pl.ds(pl.multiple_of((1 - core) * HALF, HALF), HALF)
    for dst, a, b, slot in (
        (v_out, mine, got, 0), (o_out, mine, got, 1), (q_out, mine_qk, got_qk, 0), (k_out, mine_qk, got_qk, 1),
    ):
        dst[here, :] = a[slot]
        dst[there, :] = b[slot]


def rotate(x, axis, size, by):
    return lax.ppermute(x, axis, [(i, (i + by) % size) for i in range(size)])


def flip(x, axis, size, by):
    return lax.ppermute(x, axis, [(i, i ^ by) for i in range(size)])


def along(x, by):
    count = NZ * NX
    return lax.ppermute(
        x, ("z", "x"), [(i, i + by) for i in range(count) if 0 <= i + by < count]
    )


def add16(a, b):
    return (a.astype(F32) + b.astype(F32)).astype(BF16)


def local(
    streams, short_filter, long_filter, hyena_grad, queries, keys, values, gain_q, gain_k, attn_grad
):
    channels = streams.shape[2]
    my_x = lax.axis_index("x")
    core = lax.axis_index("c")
    idx = jnp.stack([my_x, core]).astype(jnp.int32)

    def other_half(a):
        return lax.dynamic_slice_in_dim(a, (1 - core) * HALF, HALF, 0)

    swap_send = jnp.stack([other_half(a) for a in (keys, values, queries, attn_grad)], 0)
    other = rotate(swap_send, "c", NC, 1)
    g_own = jnp.stack([gain_q, gain_k], 0)
    g_other = rotate(g_own, "c", NC, 1)
    st = streams.transpose(1, 0, 2)
    rim = along(st[:, ROWS - 16 :], 1)

    squares = call(
        square_kernel, shape((8, 128), F32), in_specs=[SM, VM, VM, VM], out_specs=VM, moved=600000
    )(idx, keys, queries, other)
    sums = [squares] + [rotate(squares, "y", NY, d) for d in (1, 3, 2)]

    tile = 256
    grid = (channels // tile,)

    def spec(*lead):
        zeros = (0,) * len(lead)
        return pl.BlockSpec(lead + (tile,), lambda i: zeros + (i,))

    def whole(*dims):
        zeros = (0,) * len(dims)
        return pl.BlockSpec(dims, lambda i: zeros)

    sm, prod, gf = call(
        short_kernel,
        [shape((3, ROWS, channels), F32), shape((ROWS, channels), BF16), shape((ROWS, channels), BF16)],
        [pltpu.VMEM((3, 144, tile), F32)],
        grid=grid,
        in_specs=[spec(3, 128), spec(3, 16), spec(7, 3), spec(128)],
        out_specs=[spec(3, 128), spec(128), spec(128)],
        flops=6000000, moved=3500000,
    )(st, rim, short_filter, hyena_grad)
    prod_prev = along(prod, 1)
    gf_next = along(gf, -1)

    payload, rates = call(
        pack_kernel,
        [shape((8, 256, 128), BF16), shape((8, 128), F32)],
        in_specs=[SM] + [VM] * 11,
        out_specs=[VM, VM],
        moved=1500000,
    )(idx, keys, values, queries, attn_grad, other, g_own, g_other, *sums)
    blk = lax.all_to_all(payload, "z", 0, 0)
    kv = blk[:, 0:128].reshape(NZ * 128, HD)
    ring = [kv] + [rotate(kv, "x", NX, d) for d in (1, 2, 3)]
    pair = [rotate(a, "c", NC, 1) for a in ring]

    tables = [jnp.asarray(t) for t in transform_tables()]
    hyena_out, gs, head, tail, red = call(
        long_kernel,
        [
            shape((ROWS, channels), BF16),
            shape((3, ROWS, channels), BF16),
            shape((3, 16, channels), BF16),
            shape((3, 16, channels), F32),
            shape((192, channels), BF16),
        ],
        [pltpu.VMEM((144, tile), F32), pltpu.VMEM((3, 144, tile), F32)],
        grid=grid,
        in_specs=[
            spec(3, 128), spec(128), spec(128), spec(128), spec(128), spec(3, 128), spec(3, 16),
            spec(7, 3), spec(128),
            whole(2, 256, 128), whole(2, 256, 128), whole(2, 128, 256), whole(2, 128, 256), whole(2, 128, 256),
        ],
        out_specs=[spec(128), spec(3, 128), spec(3, 16), spec(3, 16), spec(192)],
        flops=1600000000, moved=6000000,
    )(sm, hyena_grad, prod, prod_prev, gf_next, st, rim, short_filter, long_filter, *tables)
    next_head = along(head, -1)

    quarter = red.shape[0] // NX

    def part_of(by):
        at = lax.rem(my_x + by, NX) * quarter
        return lax.dynamic_slice_in_dim(red, at, quarter, 0)

    chunk = part_of(0).astype(F32)
    for d in (1, 2, 3):
        chunk = chunk + rotate(part_of(d), "x", NX, d).astype(F32)
    chunk = chunk.astype(BF16)
    for by in (1, 2, 4):
        chunk = add16(chunk, flip(chunk, "z", NZ, by))
    full = jnp.zeros((NX, quarter, channels), F32)
    for d in range(NX):
        piece = chunk if d == 0 else rotate(chunk, "x", NX, d)
        full = lax.dynamic_update_slice_in_dim(
            full, piece.astype(F32)[None], lax.rem(my_x + NX - d, NX), 0
        )
    full = full.reshape(NX * quarter, channels)
    grad_long = full[0:128]
    grad_short = full[128:152].reshape(3, 8, channels)[:, 0:7].transpose(1, 0, 2)

    keep, gkeep, csend, osend = call(
        attention_kernel,
        [
            shape((4096, 128), F32), shape((8, 128), F32), shape((4112, 128), BF16),
            shape((8, 128, 128), BF16),
        ],
        [
            pltpu.VMEM((8, 512, 128), BF16), pltpu.VMEM((8, 512, 128), BF16),
            pltpu.VMEM((512, 128), BF16), pltpu.VMEM((512, 128), BF16),
            pltpu.VMEM((8, 512, 512), F32), pltpu.VMEM((8, 512, 512), BF16),
        ],
        in_specs=[SM] + [VM] * 9,
        out_specs=[VM] * 4,
        flops=6000000000, moved=7000000, exps=1300000,
    )(idx, blk, *ring, *pair)
    from_core = rotate(csend, "c", NC, 1)
    s0, g0, s1, s2, s3 = call(
        core_sum_kernel,
        [shape((1024, 128), F32), shape((8, 128), F32)] + [shape((1040, 128), BF16)] * 3,
        in_specs=[SM] + [VM] * 3,
        out_specs=[VM] * 5,
        moved=4000000,
    )(idx, keep, gkeep, from_core)
    rest = [rotate(s, "x", NX, d) for d, s in ((1, s1), (2, s2), (3, s3))]
    outgoing = call(
        ring_sum_kernel, shape((8, 272, 128), BF16), in_specs=[VM] * 6, out_specs=VM, moved=2000000
    )(s0, g0, *rest, osend)
    back = lax.all_to_all(outgoing, "z", 0, 0)
    half_shape = shape((2, HALF, 512), BF16)
    part, gain_grads, mine, send = call(
        inner_kernel,
        [shape((8, 128), F32), shape((2, 512), F32), half_shape, half_shape],
        in_specs=[SM] + [VM] * 6,
        out_specs=[VM] * 4,
        moved=1500000,
    )(idx, back, keys, queries, other, g_own, g_other)
    parts = [part] + [rotate(part, "y", NY, d) for d in (1, 3, 2)]
    got = rotate(send, "c", NC, 1)
    mine_qk, send_qk = call(
        norm_kernel,
        [half_shape, half_shape],
        in_specs=[SM] + [VM] * 11,
        out_specs=[VM] * 2,
        moved=1500000,
    )(idx, back, keys, queries, other, g_own, g_other, rates, *parts)
    got_qk = rotate(send_qk, "c", NC, 1)
    grad_v, attn_out, grad_q, grad_k = call(
        join_kernel,
        [shape((ROWS, 512), BF16)] * 4,
        in_specs=[SM] + [VM] * 4,
        out_specs=[VM] * 4,
        moved=1000000,
    )(idx, mine, got, mine_qk, got_qk)

    after = next_head.astype(F32)
    extra = jnp.zeros((3, 16, channels), F32)
    for j in range(1, 7):
        moved = jnp.pad(after[:, 0:j], ((0, 0), (16 - j, 0), (0, 0)))
        extra = extra + short_filter[j][:, None, :] * moved
    last = (tail + extra).astype(BF16)
    grad_streams = jnp.concatenate([gs[:, 0:112], last], 1).transpose(1, 0, 2)
    return (
        hyena_out, grad_streams, grad_short, grad_long, attn_out, grad_q, grad_k, grad_v,
        gain_grads[0], gain_grads[1],
    )


def solution(mesh):
    fine = Mesh(mesh.devices.reshape(NZ, NX, NY, NC), ("z", "x", "y", "c"))
    ctx, tp = ("z", "x"), ("y", "c")
    return jax.shard_map(
        local,
        mesh=fine,
        in_specs=(
            P(ctx, None, tp), P(None, None, tp), P(None, tp), P(ctx, tp), P(ctx, tp),
            P(ctx, tp), P(ctx, tp), P(tp), P(tp), P(ctx, tp),
        ),
        out_specs=(
            P(ctx, tp), P(ctx, None, tp), P(None, None, tp), P(None, tp), P(ctx, tp),
            P(ctx, tp), P(ctx, tp), P(ctx, tp), P(tp), P(tp),
        ),
        check_vma=False,
    )
```

```python
import functools
import math

import jax
import jax.numpy as jnp
import numpy as np
from jax import lax
from jax.experimental import pallas as pl
from jax.experimental.pallas import tpu as pltpu
from jax.sharding import Mesh
from jax.sharding import PartitionSpec as P

HD = 128
EPS = 1e-06
MASKED = -1e30
ROWS = 128
NZ, NX, NY, NC = 8, 4, 4, 2
HALF = 64
F32 = jnp.float32
BF16 = jnp.bfloat16
MIB = 1024 * 1024


def call(kernel, outs, scratch=(), us=1.0, vmem=6, **kw):
    return pl.pallas_call(
        kernel,
        out_shape=outs,
        scratch_shapes=list(scratch),
        compiler_params=pltpu.CompilerParams(vmem_limit_bytes=vmem * MIB),
        cost_estimate=pl.CostEstimate(flops=int(us * 1.1e9), bytes_accessed=0, transcendentals=0),
        **kw,
    )


def shape(dims, dtype):
    return jax.ShapeDtypeStruct(dims, dtype)


VM = pl.BlockSpec(memory_space=pltpu.VMEM)
SM = pl.BlockSpec(memory_space=pltpu.SMEM)


def transform_tables():
    n = np.arange(256)
    k = np.arange(128) + 0.5
    angle = 2.0 * np.pi * np.outer(k, n) / 256.0
    fwd = np.concatenate([np.cos(angle), -np.sin(angle)], 0)
    inv = np.concatenate([np.cos(angle), -np.sin(angle)], 0).T / 128.0
    lag = inv[128 - np.arange(128)]
    pieces = [fwd[:, :128], fwd[:, 128:]]
    for t in (inv[128:], inv[:128], lag):
        pieces += [t[:, :128], t[:, 128:]]
    t32 = np.concatenate(pieces, 0).astype(np.float32)
    hi = t32.astype(jnp.bfloat16)
    lo = (t32 - hi.astype(np.float32)).astype(jnp.bfloat16)
    return np.stack([hi, lo])


def mm(a, b):
    return jnp.dot(a, b, preferred_element_type=F32)


def table_dot(table, at, x):
    rows = 256 if at < 512 else 128
    hi, lo = table[0, at : at + rows], table[1, at : at + rows]
    if x.dtype == BF16:
        return mm(hi, x) + mm(lo, x)
    xh = x.astype(BF16)
    xl = (x - xh.astype(F32)).astype(BF16)
    return mm(hi, xh) + mm(lo, xh) + mm(hi, xl)


def hyena_kernel(
    st, prev, second, following, hg, sf, lf, tab, after,
    out, gs, head, tail, red, ext, gm,
):
    def taps(s):
        total = None
        for j in range(7):
            term = sf[s, j : j + 1, :] * ext[s, 16 - j : 272 - j, :]
            total = term if total is None else total + term
        return total

    ext[0, 0:16] = prev[256:272].astype(F32)
    ext[0, 16:144] = st[0].astype(F32)
    ext[0, 144:272] = following[0:128].astype(F32)
    for s in (1, 2):
        ext[s, 0:16] = second[16 * s - 16 : 16 * s].astype(F32)
        ext[s, 16:144] = prev[128 * s - 128 : 128 * s].astype(F32)
        ext[s, 144:272] = st[s].astype(F32)
    gates, ones, twos = taps(0), taps(1), taps(2)
    gate, one, two = gates[0:128], ones[128:256], twos[128:256]
    prod = (ones * twos).astype(BF16)
    up = hg[...].astype(F32)
    gf = up * gate
    gf_next = (following[128:256].astype(F32) * gates[128:256]).astype(BF16)
    spec_x = table_dot(tab, 0, prod[0:128]) + table_dot(tab, 256, prod[128:256])
    spec_h = table_dot(tab, 0, lf[...])
    spec_g0 = table_dot(tab, 0, gf)
    spec_g = spec_g0 + table_dot(tab, 256, gf_next)
    xr, xi = spec_x[:128], spec_x[128:]
    hr, hi = spec_h[:128], spec_h[128:]
    filt = table_dot(tab, 512, xr * hr - xi * hi) + table_dot(tab, 640, xr * hi + xi * hr)
    out[...] = (gate * filt).astype(BF16)
    gr, gi = spec_g[:128], spec_g[128:]
    gprod = table_dot(tab, 768, gr * hr + gi * hi) + table_dot(tab, 896, gi * hr - gr * hi)
    ar, ai = spec_g0[:128], spec_g0[128:]
    glong = table_dot(tab, 1024, ar * xr + ai * xi) + table_dot(tab, 1152, ar * xi - ai * xr)
    gm[:, 128:144] = jnp.zeros_like(gm[:, 128:144])
    gm[0, 0:128] = up * filt
    gm[1, 0:128] = gprod * two
    gm[2, 0:128] = gprod * one
    rows = []
    for s in range(3):
        head[s] = gm[s, 0:16].astype(BF16)
        base = 144 if s else 16
        own = gm[s, 0:128]
        total = None
        for j in range(7):
            term = sf[s, j : j + 1, :] * gm[s, j : j + 128, :]
            total = term if total is None else total + term
            rows.append(jnp.sum(own * ext[s, base - j : base + 128 - j, :], axis=0, keepdims=True))
        rows.append(jnp.zeros_like(rows[-1]))
        gs[s] = total.astype(BF16)
        tail[s] = total[112:128]
    rows.append(jnp.zeros((40, rows[-1].shape[1]), F32))
    every = jnp.concatenate([glong] + rows, 0).astype(BF16)
    for part in range(8):
        at, col = (part % 4) * 48, (part // 4) * 128
        red[part % 4, part // 4] = every[at : at + 48, col : col + 128]


def filter_kernel(idx, p0, p1, p3, p2, long_out, short_out, done, every):
    done[...] = jnp.zeros((8, 128), F32)
    my_x = idx[0]
    for d, ref in ((0, p0), (1, p1), (2, p2), (3, p3)):
        at = pl.multiple_of(lax.rem(my_x + NX - d, NX) * 48, 48)
        for z in range(NZ):
            every[pl.ds(at, 48), z * 128 : z * 128 + 128] = ref[z].astype(F32)
    long_out[...] = every[0:128]
    for s in range(3):
        short_out[s] = every[128 + 8 * s : 135 + 8 * s]


def to_lanes(col_q, col_k):
    both = jnp.concatenate([col_q, col_k], 0)
    return jnp.transpose(jnp.broadcast_to(both, (128, 128)))[0:8]


def to_columns(lanes):
    wide = jnp.transpose(jnp.broadcast_to(lanes[0:1], (128, 128)))
    return wide[0:64, 0:1], wide[64:128, 0:1]


def lane_sum(x):
    total = x[:, 0:128]
    for h in range(1, x.shape[1] // 128):
        total = total + x[:, h * 128 : (h + 1) * 128]
    return jnp.sum(total, axis=1, keepdims=True)


def split3(x):
    high = x.astype(BF16).astype(F32)
    mid = (x - high).astype(BF16).astype(F32)
    return high, mid, x - high - mid


def halves_kernel(idx, keys, values, queries, grads, streams, hg, gq, gk, mine, send, to_next, to_prev, to_second, sems):
    core = idx[1]
    here = pl.multiple_of(core * HALF, HALF)
    there = pl.multiple_of((1 - core) * HALF, HALF)
    end = pl.ds(ROWS - 16, 16)
    pairs = [
        (streams.at[1], to_next.at[pl.ds(0, ROWS)]),
        (streams.at[2], to_next.at[pl.ds(ROWS, ROWS)]),
        (streams.at[0, end], to_next.at[pl.ds(2 * ROWS, 16)]),
        (streams.at[0], to_prev.at[pl.ds(0, ROWS)]),
        (hg, to_prev.at[pl.ds(ROWS, ROWS)]),
        (streams.at[1, end], to_second.at[pl.ds(0, 16)]),
        (streams.at[2, end], to_second.at[pl.ds(16, 16)]),
    ]
    for a, ref in enumerate((keys, values, queries, grads)):
        dst = pl.ds(a * HALF, HALF)
        pairs.append((ref.at[pl.ds(there, HALF)], send.at[dst]))
        pairs.append((ref.at[pl.ds(here, HALF)], mine.at[dst]))
    copies = [pltpu.make_async_copy(src, dst, sems.at[i]) for i, (src, dst) in enumerate(pairs)]
    for c in copies:
        c.start()
    both = jnp.concatenate([gq[...], gk[...]], 0)
    parts = list(split3(both)) + [jnp.zeros((10, 512), F32)]
    send[256:272] = jnp.concatenate(parts, 0).astype(BF16)
    for c in copies:
        c.wait()


def own_gains(gn_q, gn_k):
    return jnp.concatenate([gn_q[...], gn_k[...]], 0)


def other_gains(other):
    wide = other[256:272].astype(F32)
    return wide[0:2] + wide[2:4] + wide[4:6]


def square_kernel(mine, other, out):
    sums = []
    for slot in (2, 0):
        at = slice(slot * HALF, slot * HALF + HALF)
        a, b = mine[at].astype(F32), other[at].astype(F32)
        sums.append(lane_sum(a * a + b * b))
    out[...] = to_lanes(sums[0], sums[1])


def pack_kernel(idx, mine, other, gn_q, gn_k, s0, s1, s2, s3, h0, h1, h2, out, rates):
    core = idx[1]
    rate = lax.rsqrt((s0[...] + s1[...] + s2[...] + s3[...]) / (NY * 8 * HD) + EPS)
    rates[...] = rate
    rate_q, rate_k = to_columns(rate)
    for ref, gains, first in ((mine, own_gains(gn_q, gn_k), core * 4), (other, other_gains(other), (1 - core) * 4)):
        for h in range(4):
            cols = slice(h * 128, (h + 1) * 128)
            key, query = ref[0:64, cols].astype(F32), ref[128:192, cols].astype(F32)
            out[first + h, 0:64] = (key * rate_k * gains[1:2, cols]).astype(BF16)
            out[first + h, 64:128] = ref[64:128, cols]
            out[first + h, 128:192] = (query * rate_q * gains[0:1, cols]).astype(BF16)
            out[first + h, 192:256] = ref[192:256, cols]


def keys_kernel(blk, after, out):
    for z in range(NZ):
        out[z * 128 : z * 128 + 128] = blk[z, 0:128]


def stack_kernel(idx, a, b, c, d, red, out, *parts):
    for i, ref in enumerate((a, b, c, d)):
        out[i] = ref[...]
    for d, part in enumerate(parts):
        part[...] = red[lax.rem(idx[0] + d, NX)]


def scatter_sum_kernel(p0, p1, p2, p3, after, out, done):
    done[...] = jnp.zeros((8, 128), F32)
    total = p0[...].astype(F32) + p1[...].astype(F32) + p2[...].astype(F32) + p3[...].astype(F32)
    out[...] = total.astype(BF16)


def pair_sum_kernel(a, b, after, out, done):
    done[...] = jnp.zeros((8, 128), F32)
    out[...] = (a[...].astype(F32) + b[...].astype(F32)).astype(BF16)


def attention_kernel(
    idx, blk, mine, pair,
    keep, gkeep, csend, osend,
    k_all, v_all, q_all, d_all, s_all, w_all,
):
    my_x, core = idx[0], idx[1]
    for d in range(NX):
        xd = lax.rem(my_x + NX - d, NX)
        for ref, cc in ((mine, core), (pair, 1 - core)):
            at = pl.multiple_of(xd * 128 + cc * 64, 64)
            for z in range(NZ):
                k_all[z, pl.ds(at, 64)] = ref[d, z * 128 : z * 128 + 64]
                v_all[z, pl.ds(at, 64)] = ref[d, z * 128 + 64 : z * 128 + 128]
    for z in range(NZ):
        q_all[z * 64 : z * 64 + 64] = blk[z, 128:192]
        d_all[z * 64 : z * 64 + 64] = blk[z, 192:256]
    scale = 1.0 / math.sqrt(HD)
    power = scale * math.log2(math.e)
    base = my_x * 128 + core * 64
    nt = (((1,), (1,)), ((), ()))
    tn = (((0,), (0,)), ((), ()))

    def first(kz):
        return (kz // 2) * 128

    key_row = lax.broadcasted_iota(jnp.int32, (512, 128), 0)
    lane = lax.broadcasted_iota(jnp.int32, (512, 128), 1)
    query_row = (lane // 64) * 512 + base + lane % 64

    row_max = jnp.full((1, 512), MASKED, F32)
    for kz in range(NZ):
        lo = first(kz)
        sc = lax.dot_general(k_all[kz], q_all[lo:512], nt, preferred_element_type=F32)
        diag = jnp.where(key_row + (kz % 2) * 512 <= query_row, sc[:, 0:128], MASKED)
        sc = diag if lo == 384 else jnp.concatenate([diag, sc[:, 128:]], 1)
        s_all[kz, :, lo:512] = sc
        top = jnp.max(sc, axis=0, keepdims=True)
        top = jnp.maximum(row_max[:, lo:], top)
        row_max = top if lo == 0 else jnp.concatenate([row_max[:, :lo], top], 1)
    row_sum = jnp.zeros((1, 512), F32)
    for kz in range(NZ):
        lo = first(kz)
        p = jnp.exp2((s_all[kz, :, lo:512] - row_max[:, lo:]) * power)
        s_all[kz, :, lo:512] = p
        more = row_sum[:, lo:] + jnp.sum(p, axis=0, keepdims=True)
        row_sum = more if lo == 0 else jnp.concatenate([row_sum[:, :lo], more], 1)
    inv = 1.0 / row_sum
    out_t = jnp.zeros((128, 512), F32)
    for kz in range(NZ):
        lo = first(kz)
        w = (s_all[kz, :, lo:512] * inv[:, lo:]).astype(BF16)
        w_all[kz, :, lo:512] = w
        piece = out_t[:, lo:] + lax.dot_general(v_all[kz], w, tn, preferred_element_type=F32)
        out_t = piece if lo == 0 else jnp.concatenate([out_t[:, :lo], piece], 1)
    out_b = jnp.transpose(out_t).astype(BF16)
    spread_col = jnp.sum(out_b.astype(F32) * d_all[...].astype(F32), axis=1, keepdims=True)
    spread = jnp.transpose(jnp.broadcast_to(spread_col, (512, 128)))[0:1]
    grad_qt = jnp.zeros((128, 512), F32)
    gain_k = jnp.zeros((1, 128), F32)
    for kz in range(NZ):
        lo = first(kz)
        w = w_all[kz, :, lo:512]
        dp = lax.dot_general(v_all[kz], d_all[lo:512], nt, preferred_element_type=F32)
        ds = (w.astype(F32) * (dp - spread[:, lo:])).astype(BF16)
        grad_v = mm(w, d_all[lo:512])
        grad_k = mm(ds, q_all[lo:512]) * scale
        piece = grad_qt[:, lo:] + lax.dot_general(k_all[kz], ds, tn, preferred_element_type=F32)
        grad_qt = piece if lo == 0 else jnp.concatenate([grad_qt[:, :lo], piece], 1)
        gain_k = gain_k + jnp.sum(grad_k * k_all[kz].astype(F32), axis=0, keepdims=True)
        for xx in range(NX):
            at = xx * 1024 + kz * 128
            for arr, val in enumerate((grad_k, grad_v)):
                dst = slice(at + arr * 64, at + arr * 64 + 64)
                half0 = val[xx * 128 : xx * 128 + 64]
                half1 = val[xx * 128 + 64 : xx * 128 + 128]
                keep[dst] = jnp.where(core == 0, half0, half1)
                csend[dst] = jnp.where(core == 0, half1, half0).astype(BF16)
    grad_q = jnp.transpose(grad_qt) * scale
    gain_q = jnp.sum(grad_q * q_all[...].astype(F32), axis=0, keepdims=True)
    gains = jnp.concatenate([gain_q, gain_k, jnp.zeros((6, 128), F32)], 0)
    gkeep[...] = gains
    high = gains.astype(BF16).astype(F32)
    csend[4096:4112] = jnp.concatenate([high, gains - high], 0).astype(BF16)
    for z in range(NZ):
        osend[z, 0:64] = out_b[z * 64 : z * 64 + 64]
        osend[z, 64:128] = grad_q[z * 64 : z * 64 + 64].astype(BF16)


def gains_of(rows16):
    wide = rows16.astype(F32)
    return wide[0:8] + wide[8:16]


def core_sum_kernel(idx, keep, gkeep, other, after, s0, g0, s1, s2, s3):
    my_x = idx[0]
    gains = gkeep[...] + gains_of(other[4096:4112])
    g0[...] = gains
    high = gains.astype(BF16).astype(F32)
    rows = jnp.concatenate([high, gains - high], 0).astype(BF16)
    for d, ref in enumerate((s0, s1, s2, s3)):
        at = pl.multiple_of(lax.rem(my_x + d, NX) * 1024, 1024)
        total = keep[pl.ds(at, 1024)] + other[pl.ds(at, 1024)].astype(F32)
        ref[0:1024] = total.astype(ref.dtype)
        if d:
            ref[1024:1040] = rows


def ring_sum_kernel(s0, g0, r1, r2, r3, osend, after, out, done):
    done[...] = g0[...]
    gains = g0[...] + gains_of(r1[1024:1040]) + gains_of(r2[1024:1040]) + gains_of(r3[1024:1040])
    high = gains.astype(BF16).astype(F32)
    rows = jnp.concatenate([high, gains - high], 0).astype(BF16)
    for z in range(NZ):
        at = slice(z * 128, z * 128 + 128)
        total = s0[at] + r1[at].astype(F32) + r2[at].astype(F32) + r3[at].astype(F32)
        out[z, 0:128] = total.astype(BF16)
        out[z, 128:256] = osend[z]
        out[z, 256:272] = rows


def inner_kernel(idx, back, mine, other, gn_q, gn_k, after, part, gains_q, gains_k):
    core = idx[1]
    sum_q = jnp.zeros((64, 128), F32)
    sum_k = jnp.zeros((64, 128), F32)
    for ref, gain, first in ((mine, own_gains(gn_q, gn_k), core * 4), (other, other_gains(other), (1 - core) * 4)):
        for h in range(4):
            cols = slice(h * 128, (h + 1) * 128)
            gk = back[first + h, 0:64].astype(F32)
            gq = back[first + h, 192:256].astype(F32)
            sum_q = sum_q + gq * gain[0:1, cols] * ref[128:192, cols].astype(F32)
            sum_k = sum_k + gk * gain[1:2, cols] * ref[0:64, cols].astype(F32)
    part[...] = to_lanes(
        jnp.sum(sum_q, axis=1, keepdims=True), jnp.sum(sum_k, axis=1, keepdims=True)
    )
    for h in range(4):
        cols = slice(h * 128, (h + 1) * 128)
        got = gains_of(back[core * 4 + h, 256:272])
        gains_q[0:1, cols] = got[0:1] / gn_q[:, cols]
        gains_k[0:1, cols] = got[1:2] / gn_k[:, cols]


def norm_kernel(idx, back, mine, other, gn_q, gn_k, rates, p0, p1, p2, p3, keep, send):
    core = idx[1]
    rate_q, rate_k = to_columns(rates[...])
    inner_q, inner_k = to_columns(p0[...] + p1[...] + p2[...] + p3[...])
    width = NY * 8 * HD
    coef_q = rate_q * rate_q * rate_q * inner_q / width
    coef_k = rate_k * rate_k * rate_k * inner_k / width
    for ref, gain, first, dst in (
        (mine, own_gains(gn_q, gn_k), core * 4, keep), (other, other_gains(other), (1 - core) * 4, send)
    ):
        for h in range(4):
            cols = slice(h * 128, (h + 1) * 128)
            gk = back[first + h, 0:64].astype(F32)
            gq = back[first + h, 192:256].astype(F32)
            raw_k, raw_q = ref[0:64, cols].astype(F32), ref[128:192, cols].astype(F32)
            dst[0, :, cols] = (rate_q * (gq * gain[0:1, cols]) - raw_q * coef_q).astype(BF16)
            dst[1, :, cols] = (rate_k * (gk * gain[1:2, cols]) - raw_k * coef_k).astype(BF16)
            dst[2, :, cols] = back[first + h, 64:128]
            dst[3, :, cols] = back[first + h, 128:192]


def join_kernel(idx, mine, got, q_out, k_out, v_out, o_out):
    core = idx[1]
    here = pl.ds(pl.multiple_of(core * HALF, HALF), HALF)
    there = pl.ds(pl.multiple_of((1 - core) * HALF, HALF), HALF)
    for slot, dst in enumerate((q_out, k_out, v_out, o_out)):
        dst[here, :] = mine[slot]
        dst[there, :] = got[slot]


def rotate(x, axis, size, by):
    return lax.ppermute(x, axis, [(i, (i + by) % size) for i in range(size)])


def flip(x, axis, size, by):
    return lax.ppermute(x, axis, [(i, i ^ by) for i in range(size)])


def along(x, by):
    count = NZ * NX
    return lax.ppermute(
        x, ("z", "x"), [(i, i + by) for i in range(count) if 0 <= i + by < count]
    )


def add16(a, b):
    return (a.astype(F32) + b.astype(F32)).astype(BF16)


def local(
    streams, short_filter, long_filter, hyena_grad, queries, keys, values, gain_q, gain_k, attn_grad
):
    channels = streams.shape[2]
    my_x = lax.axis_index("x")
    core = lax.axis_index("c")
    idx = jnp.stack([my_x, core, lax.axis_index("z")]).astype(jnp.int32)

    gains = (gain_q.reshape(1, 512), gain_k.reshape(1, 512))
    ANY = pl.BlockSpec(memory_space=pl.ANY)
    tab = jnp.asarray(transform_tables())
    st = streams.transpose(1, 0, 2)
    sf = short_filter.transpose(1, 0, 2)
    mine, send, to_next, to_prev, to_second = call(
        halves_kernel,
        [
            shape((256, 512), BF16), shape((272, 512), BF16), shape((272, channels), BF16),
            shape((256, channels), BF16), shape((32, channels), BF16),
        ],
        [pltpu.SemaphoreType.DMA((15,))],
        in_specs=[SM] + [ANY] * 6 + [VM] * 2,
        out_specs=[VM] * 5,
        us=1.0,
        vmem=60,
    )(idx, keys, values, queries, attn_grad, st, hyena_grad, *gains)
    other = rotate(send, "c", NC, 1)
    second = along(to_second, 2)
    prev = along(to_next, 1)
    following = along(to_prev, -1)

    squares = call(square_kernel, shape((8, 128), F32), in_specs=[VM, VM], out_specs=VM, us=0.7)(mine, other)
    sums = [squares] + [rotate(squares, "y", NY, d) for d in (1, 3, 2)]
    payload, rates = call(
        pack_kernel,
        [shape((8, 256, 128), BF16), shape((8, 128), F32)],
        in_specs=[SM] + [VM] * 8 + [ANY] * 3,
        out_specs=[VM, VM],
        us=1.5,
    )(idx, mine, other, *gains, *sums, prev, following, second)
    blk = lax.all_to_all(payload, "z", 0, 0)

    tile = 256
    grid = (channels // tile,)

    def spec(*lead):
        zeros = (0,) * len(lead)
        return pl.BlockSpec(lead + (tile,), lambda i: zeros + (i,))

    def whole(*dims):
        zeros = (0,) * len(dims)
        return pl.BlockSpec(dims, lambda i: zeros)

    hyena_out, gs, head, tail, red = call(
        hyena_kernel,
        [
            shape((ROWS, channels), BF16),
            shape((3, ROWS, channels), BF16),
            shape((3, 16, channels), BF16),
            shape((3, 16, channels), F32),
            shape((NX, NZ, 48, 128), BF16),
        ],
        [pltpu.VMEM((3, 272, tile), F32), pltpu.VMEM((3, 144, tile), F32)],
        grid=grid,
        in_specs=[
            spec(3, 128), spec(272), spec(32), spec(256), spec(128),
            spec(3, 7), spec(128), whole(2, 1280, 128), ANY,
        ],
        out_specs=[
            spec(128), spec(3, 128), spec(3, 16), spec(3, 16), pl.BlockSpec((NX, 2, 48, 128), lambda i: (0, i, 0, 0)),
        ],
        us=11.0, vmem=56,
    )(st, prev, second, following, hyena_grad, sf, long_filter, tab, rates)
    next_head = along(head, -1)

    kv = call(
        keys_kernel, shape((NZ * 128, HD), BF16), in_specs=[VM, ANY], out_specs=VM, us=0.5
    )(blk, tail)
    piece_shape = shape((NZ, 48, 128), BF16)
    ring, *parts = call(
        stack_kernel,
        [shape((NX, NZ * 128, HD), BF16)] + [piece_shape] * NX,
        in_specs=[SM] + [VM] * 5, out_specs=[VM] * 5, us=1.0,
    )(idx, kv, *[rotate(kv, "x", NX, d) for d in (1, 2, 3)], red)
    parts = parts[:1] + [rotate(parts[d], "x", NX, d) for d in (1, 2, 3)]
    pair = rotate(ring, "c", NC, 1)

    keep, gkeep, csend, osend = call(
        attention_kernel,
        [
            shape((4096, 128), F32), shape((8, 128), F32), shape((4112, 128), BF16),
            shape((8, 128, 128), BF16),
        ],
        [
            pltpu.VMEM((8, 512, 128), BF16), pltpu.VMEM((8, 512, 128), BF16),
            pltpu.VMEM((512, 128), BF16), pltpu.VMEM((512, 128), BF16),
            pltpu.VMEM((8, 512, 512), F32), pltpu.VMEM((8, 512, 512), BF16),
        ],
        in_specs=[SM] + [VM] * 3,
        out_specs=[VM] * 4,
        us=7.0, vmem=28,
    )(idx, blk, ring, pair)
    from_core = rotate(csend, "c", NC, 1)

    token = shape((8, 128), F32)
    piece, scattered = call(
        scatter_sum_kernel, [piece_shape, token], in_specs=[VM] * 4 + [ANY], out_specs=[VM] * 2, us=0.6
    )(*parts, gkeep)
    s0, g0, s1, s2, s3 = call(
        core_sum_kernel,
        [shape((1024, 128), F32), shape((8, 128), F32)] + [shape((1040, 128), BF16)] * 3,
        in_specs=[SM] + [VM] * 3 + [ANY],
        out_specs=[VM] * 5,
        us=1.0,
    )(idx, keep, gkeep, from_core, scattered)
    rest = [rotate(s, "x", NX, d) for d, s in ((1, s1), (2, s2), (3, s3))]
    for by in (1, 2, 4):
        piece, added = call(
            pair_sum_kernel, [piece_shape, token], in_specs=[VM] * 2 + [ANY], out_specs=[VM] * 2, us=0.6
        )(piece, flip(piece, "z", NZ, by), g0)
    outgoing, summed = call(
        ring_sum_kernel,
        [shape((8, 272, 128), BF16), shape((8, 128), F32)],
        in_specs=[VM] * 6 + [ANY], out_specs=[VM] * 2, us=1.0,
    )(s0, g0, *rest, osend, added)
    back = lax.all_to_all(outgoing, "z", 0, 0)

    pieces = [piece] + [rotate(piece, "x", NX, d) for d in (1, 3, 2)]
    grad_long, short_rows, filters = call(
        filter_kernel,
        [shape((128, channels), F32), shape((3, 7, channels), F32), shape((8, 128), F32)],
        in_specs=[SM] + [VM] * 4, out_specs=[VM] * 3, scratch=[pltpu.VMEM((192, channels), F32)],
        us=1.0,
    )(idx, *pieces)
    grad_short = short_rows.transpose(1, 0, 2)
    half_shape = shape((4, HALF, 512), BF16)
    part, gain_grad_q, gain_grad_k = call(
        inner_kernel,
        [shape((8, 128), F32), shape((1, 512), F32), shape((1, 512), F32)],
        in_specs=[SM] + [VM] * 5 + [ANY],
        out_specs=[VM] * 3,
        us=1.0,
    )(idx, back, mine, other, *gains, filters)
    parts = [part] + [rotate(part, "y", NY, d) for d in (1, 3, 2)]
    kept, send = call(
        norm_kernel,
        [half_shape, half_shape],
        in_specs=[SM] + [VM] * 10,
        out_specs=[VM] * 2,
        us=1.0,
    )(idx, back, mine, other, *gains, rates, *parts)
    got = rotate(send, "c", NC, 1)
    grad_q, grad_k, grad_v, attn_out = call(
        join_kernel,
        [shape((ROWS, 512), BF16)] * 4,
        in_specs=[SM] + [VM] * 2,
        out_specs=[VM] * 4,
        us=1.0,
    )(idx, kept, got)

    after = next_head.astype(F32)
    extra = jnp.zeros((3, 16, channels), F32)
    for j in range(1, 7):
        moved = jnp.pad(after[:, 0:j], ((0, 0), (16 - j, 0), (0, 0)))
        extra = extra + sf[:, j : j + 1] * moved
    last = (tail + extra).astype(BF16)
    grad_streams = jnp.concatenate([gs[:, 0:112], last], 1).transpose(1, 0, 2)
    return (
        hyena_out, grad_streams, grad_short, grad_long, attn_out, grad_q, grad_k, grad_v,
        gain_grad_q.reshape(512), gain_grad_k.reshape(512),
    )


def solution(mesh):
    fine = Mesh(mesh.devices.reshape(NZ, NX, NY, NC), ("z", "x", "y", "c"))
    ctx, tp = ("z", "x"), ("y", "c")
    return jax.shard_map(
        local,
        mesh=fine,
        in_specs=(
            P(ctx, None, tp), P(None, None, tp), P(None, tp), P(ctx, tp), P(ctx, tp),
            P(ctx, tp), P(ctx, tp), P(tp), P(tp), P(ctx, tp),
        ),
        out_specs=(
            P(ctx, tp), P(ctx, None, tp), P(None, None, tp), P(None, tp), P(ctx, tp),
            P(ctx, tp), P(ctx, tp), P(ctx, tp), P(tp), P(tp),
        ),
        check_vma=False,
    )
```

```python
import functools
import math

import jax
import jax.numpy as jnp
import numpy as np
from jax import lax
from jax.experimental import pallas as pl
from jax.experimental.pallas import tpu as pltpu
from jax.sharding import Mesh
from jax.sharding import PartitionSpec as P

HD = 128
EPS = 1e-06
MASKED = -1e30
ROWS = 128
NZ, NX, NY, NC = 8, 4, 4, 2
HALF = 64
F32 = jnp.float32
BF16 = jnp.bfloat16
MIB = 1024 * 1024


def call(kernel, outs, scratch=(), us=1.0, vmem=6, **kw):
    return pl.pallas_call(
        kernel,
        out_shape=outs,
        scratch_shapes=list(scratch),
        compiler_params=pltpu.CompilerParams(vmem_limit_bytes=vmem * MIB),
        cost_estimate=pl.CostEstimate(flops=int(us * 1.1e9), bytes_accessed=0, transcendentals=0),
        **kw,
    )


def shape(dims, dtype):
    return jax.ShapeDtypeStruct(dims, dtype)


VM = pl.BlockSpec(memory_space=pltpu.VMEM)
SM = pl.BlockSpec(memory_space=pltpu.SMEM)


def transform_tables():
    n = np.arange(256)
    k = np.arange(128) + 0.5
    angle = 2.0 * np.pi * np.outer(k, n) / 256.0
    fwd = np.concatenate([np.cos(angle), -np.sin(angle)], 0)
    inv = np.concatenate([np.cos(angle), -np.sin(angle)], 0).T / 128.0
    lag = inv[128 - np.arange(128)]
    pieces = [fwd[:, :128], fwd[:, 128:]]
    for t in (inv[128:], inv[:128], lag):
        pieces += [t[:, :128], t[:, 128:]]
    t32 = np.concatenate(pieces, 0).astype(np.float32)
    hi = t32.astype(jnp.bfloat16)
    lo = (t32 - hi.astype(np.float32)).astype(jnp.bfloat16)
    return np.stack([hi, lo])


def mm(a, b):
    return jnp.dot(a, b, preferred_element_type=F32)


def table_dot(table, at, x):
    rows = 256 if at < 512 else 128
    hi, lo = table[0, at : at + rows], table[1, at : at + rows]
    if x.dtype == BF16:
        return mm(hi, x) + mm(lo, x)
    xh = x.astype(BF16)
    xl = (x - xh.astype(F32)).astype(BF16)
    return mm(hi, xh) + mm(lo, xh) + mm(hi, xl)


def hyena_kernel(
    st, prev, second, following, hg, sf, lf, tab, after,
    out, gs, head, tail, red, done, ext, gm,
):
    done[...] = jnp.zeros((8, 128), F32)
    def taps(s):
        total = None
        for j in range(7):
            term = sf[s, j : j + 1, :] * ext[s, 16 - j : 272 - j, :]
            total = term if total is None else total + term
        return total

    ext[0, 0:16] = prev[256:272].astype(F32)
    ext[0, 16:144] = st[0].astype(F32)
    ext[0, 144:272] = following[0:128].astype(F32)
    for s in (1, 2):
        ext[s, 0:16] = second[16 * s - 16 : 16 * s].astype(F32)
        ext[s, 16:144] = prev[128 * s - 128 : 128 * s].astype(F32)
        ext[s, 144:272] = st[s].astype(F32)
    gates, ones, twos = taps(0), taps(1), taps(2)
    gate, one, two = gates[0:128], ones[128:256], twos[128:256]
    prod = (ones * twos).astype(BF16)
    up = hg[...].astype(F32)
    gf = up * gate
    gf_next = (following[128:256].astype(F32) * gates[128:256]).astype(BF16)
    spec_x = table_dot(tab, 0, prod[0:128]) + table_dot(tab, 256, prod[128:256])
    spec_h = table_dot(tab, 0, lf[...])
    spec_g0 = table_dot(tab, 0, gf)
    spec_g = spec_g0 + table_dot(tab, 256, gf_next)
    xr, xi = spec_x[:128], spec_x[128:]
    hr, hi = spec_h[:128], spec_h[128:]
    filt = table_dot(tab, 512, xr * hr - xi * hi) + table_dot(tab, 640, xr * hi + xi * hr)
    out[...] = (gate * filt).astype(BF16)
    gr, gi = spec_g[:128], spec_g[128:]
    gprod = table_dot(tab, 768, gr * hr + gi * hi) + table_dot(tab, 896, gi * hr - gr * hi)
    ar, ai = spec_g0[:128], spec_g0[128:]
    glong = table_dot(tab, 1024, ar * xr + ai * xi) + table_dot(tab, 1152, ar * xi - ai * xr)
    gm[:, 128:144] = jnp.zeros_like(gm[:, 128:144])
    gm[0, 0:128] = up * filt
    gm[1, 0:128] = gprod * two
    gm[2, 0:128] = gprod * one
    rows = []
    for s in range(3):
        head[s] = gm[s, 0:16].astype(BF16)
        base = 144 if s else 16
        own = gm[s, 0:128]
        total = None
        for j in range(7):
            term = sf[s, j : j + 1, :] * gm[s, j : j + 128, :]
            total = term if total is None else total + term
            rows.append(jnp.sum(own * ext[s, base - j : base + 128 - j, :], axis=0, keepdims=True))
        rows.append(jnp.zeros_like(rows[-1]))
        gs[s] = total.astype(BF16)
        tail[s] = total[112:128]
    rows.append(jnp.zeros((40, rows[-1].shape[1]), F32))
    every = jnp.concatenate([glong] + rows, 0).astype(BF16)
    for part in range(8):
        at, col = (part % 4) * 48, (part // 4) * 128
        red[part % 4, part // 4] = every[at : at + 48, col : col + 128]


def filter_kernel(idx, p0, p1, p3, p2, long_out, short_out, done, every):
    done[...] = jnp.zeros((8, 128), F32)
    my_x = idx[0]
    for d, ref in ((0, p0), (1, p1), (2, p2), (3, p3)):
        at = pl.multiple_of(lax.rem(my_x + NX - d, NX) * 48, 48)
        for z in range(NZ):
            every[pl.ds(at, 48), z * 128 : z * 128 + 128] = ref[z].astype(F32)
    long_out[...] = every[0:128]
    for s in range(3):
        short_out[s] = every[128 + 8 * s : 135 + 8 * s]


def to_lanes(col_q, col_k):
    both = jnp.concatenate([col_q, col_k], 0)
    return jnp.transpose(jnp.broadcast_to(both, (128, 128)))[0:8]


def to_columns(lanes):
    wide = jnp.transpose(jnp.broadcast_to(lanes[0:1], (128, 128)))
    return wide[0:64, 0:1], wide[64:128, 0:1]


def lane_sum(x):
    total = x[:, 0:128]
    for h in range(1, x.shape[1] // 128):
        total = total + x[:, h * 128 : (h + 1) * 128]
    return jnp.sum(total, axis=1, keepdims=True)


def split3(x):
    high = x.astype(BF16).astype(F32)
    mid = (x - high).astype(BF16).astype(F32)
    return high, mid, x - high - mid


def halves_kernel(idx, keys, values, queries, grads, streams, hg, gq, gk, mine, send, to_next, to_prev, to_second, sems):
    core = idx[1]
    here = pl.multiple_of(core * HALF, HALF)
    there = pl.multiple_of((1 - core) * HALF, HALF)
    end = pl.ds(ROWS - 16, 16)
    pairs = [
        (streams.at[1], to_next.at[pl.ds(0, ROWS)]),
        (streams.at[2], to_next.at[pl.ds(ROWS, ROWS)]),
        (streams.at[0, end], to_next.at[pl.ds(2 * ROWS, 16)]),
        (streams.at[0], to_prev.at[pl.ds(0, ROWS)]),
        (hg, to_prev.at[pl.ds(ROWS, ROWS)]),
        (streams.at[1, end], to_second.at[pl.ds(0, 16)]),
        (streams.at[2, end], to_second.at[pl.ds(16, 16)]),
    ]
    for a, ref in enumerate((keys, values, queries, grads)):
        dst = pl.ds(a * HALF, HALF)
        pairs.append((ref.at[pl.ds(there, HALF)], send.at[dst]))
        pairs.append((ref.at[pl.ds(here, HALF)], mine.at[dst]))
    copies = [pltpu.make_async_copy(src, dst, sems.at[i]) for i, (src, dst) in enumerate(pairs)]
    for c in copies:
        c.start()
    both = jnp.concatenate([gq[...], gk[...]], 0)
    parts = list(split3(both)) + [jnp.zeros((10, 512), F32)]
    send[256:272] = jnp.concatenate(parts, 0).astype(BF16)
    for c in copies:
        c.wait()


def own_gains(gn_q, gn_k):
    return jnp.concatenate([gn_q[...], gn_k[...]], 0)


def other_gains(other):
    wide = other[256:272].astype(F32)
    return wide[0:2] + wide[2:4] + wide[4:6]


def square_kernel(mine, other, out):
    sums = []
    for slot in (2, 0):
        at = slice(slot * HALF, slot * HALF + HALF)
        a, b = mine[at].astype(F32), other[at].astype(F32)
        sums.append(lane_sum(a * a + b * b))
    out[...] = to_lanes(sums[0], sums[1])


def pack_kernel(idx, mine, other, gn_q, gn_k, s0, s1, s2, s3, h0, h1, h2, out, rates):
    core = idx[1]
    rate = lax.rsqrt((s0[...] + s1[...] + s2[...] + s3[...]) / (NY * 8 * HD) + EPS)
    rates[...] = rate
    rate_q, rate_k = to_columns(rate)
    for ref, gains, first in ((mine, own_gains(gn_q, gn_k), core * 4), (other, other_gains(other), (1 - core) * 4)):
        for h in range(4):
            cols = slice(h * 128, (h + 1) * 128)
            key, query = ref[0:64, cols].astype(F32), ref[128:192, cols].astype(F32)
            out[first + h, 0:64] = (key * rate_k * gains[1:2, cols]).astype(BF16)
            out[first + h, 64:128] = ref[64:128, cols]
            out[first + h, 128:192] = (query * rate_q * gains[0:1, cols]).astype(BF16)
            out[first + h, 192:256] = ref[192:256, cols]


def keys_kernel(blk, after, out):
    for z in range(NZ):
        out[z * 128 : z * 128 + 128] = blk[z, 0:128]


def stack_kernel(idx, a, c, b, d, red, out, *parts):
    for i, ref in enumerate((a, b, c, d)):
        out[i] = ref[...]
    for d, part in enumerate(parts):
        part[...] = red[lax.rem(idx[0] + d, NX)]


def scatter_sum_kernel(p0, p1, p2, p3, after, out, done):
    done[...] = jnp.zeros((8, 128), F32)
    total = p0[...].astype(F32) + p1[...].astype(F32) + p2[...].astype(F32) + p3[...].astype(F32)
    out[...] = total.astype(BF16)


def pair_sum_kernel(a, b, after, out, done):
    done[...] = jnp.zeros((8, 128), F32)
    out[...] = (a[...].astype(F32) + b[...].astype(F32)).astype(BF16)


def attention_kernel(
    idx, blk, mine, pair,
    keep, gkeep, csend, osend,
    k_all, v_all, q_all, d_all, s_all, w_all,
):
    my_x, core = idx[0], idx[1]
    for d in range(NX):
        xd = lax.rem(my_x + NX - d, NX)
        for ref, cc in ((mine, core), (pair, 1 - core)):
            at = pl.multiple_of(xd * 128 + cc * 64, 64)
            for z in range(NZ):
                k_all[z, pl.ds(at, 64)] = ref[d, z * 128 : z * 128 + 64]
                v_all[z, pl.ds(at, 64)] = ref[d, z * 128 + 64 : z * 128 + 128]
    for z in range(NZ):
        q_all[z * 64 : z * 64 + 64] = blk[z, 128:192]
        d_all[z * 64 : z * 64 + 64] = blk[z, 192:256]
    scale = 1.0 / math.sqrt(HD)
    power = scale * math.log2(math.e)
    base = my_x * 128 + core * 64
    nt = (((1,), (1,)), ((), ()))
    tn = (((0,), (0,)), ((), ()))

    def first(kz):
        return (kz // 2) * 128

    key_row = lax.broadcasted_iota(jnp.int32, (512, 128), 0)
    lane = lax.broadcasted_iota(jnp.int32, (512, 128), 1)
    query_row = (lane // 64) * 512 + base + lane % 64

    row_max = jnp.full((1, 512), MASKED, F32)
    for kz in range(NZ):
        lo = first(kz)
        sc = lax.dot_general(k_all[kz], q_all[lo:512], nt, preferred_element_type=F32)
        diag = jnp.where(key_row + (kz % 2) * 512 <= query_row, sc[:, 0:128], MASKED)
        sc = diag if lo == 384 else jnp.concatenate([diag, sc[:, 128:]], 1)
        s_all[kz, :, lo:512] = sc
        top = jnp.max(sc, axis=0, keepdims=True)
        top = jnp.maximum(row_max[:, lo:], top)
        row_max = top if lo == 0 else jnp.concatenate([row_max[:, :lo], top], 1)
    row_sum = jnp.zeros((1, 512), F32)
    for kz in range(NZ):
        lo = first(kz)
        p = jnp.exp2((s_all[kz, :, lo:512] - row_max[:, lo:]) * power)
        s_all[kz, :, lo:512] = p
        more = row_sum[:, lo:] + jnp.sum(p, axis=0, keepdims=True)
        row_sum = more if lo == 0 else jnp.concatenate([row_sum[:, :lo], more], 1)
    inv = 1.0 / row_sum
    out_t = jnp.zeros((128, 512), F32)
    for kz in range(NZ):
        lo = first(kz)
        w = (s_all[kz, :, lo:512] * inv[:, lo:]).astype(BF16)
        w_all[kz, :, lo:512] = w
        piece = out_t[:, lo:] + lax.dot_general(v_all[kz], w, tn, preferred_element_type=F32)
        out_t = piece if lo == 0 else jnp.concatenate([out_t[:, :lo], piece], 1)
    out_b = jnp.transpose(out_t).astype(BF16)
    spread_col = jnp.sum(out_b.astype(F32) * d_all[...].astype(F32), axis=1, keepdims=True)
    spread = jnp.transpose(jnp.broadcast_to(spread_col, (512, 128)))[0:1]
    grad_qt = jnp.zeros((128, 512), F32)
    gain_k = jnp.zeros((1, 128), F32)
    for kz in range(NZ):
        lo = first(kz)
        w = w_all[kz, :, lo:512]
        dp = lax.dot_general(v_all[kz], d_all[lo:512], nt, preferred_element_type=F32)
        ds = (w.astype(F32) * (dp - spread[:, lo:])).astype(BF16)
        grad_v = mm(w, d_all[lo:512])
        grad_k = mm(ds, q_all[lo:512]) * scale
        piece = grad_qt[:, lo:] + lax.dot_general(k_all[kz], ds, tn, preferred_element_type=F32)
        grad_qt = piece if lo == 0 else jnp.concatenate([grad_qt[:, :lo], piece], 1)
        gain_k = gain_k + jnp.sum(grad_k * k_all[kz].astype(F32), axis=0, keepdims=True)
        for xx in range(NX):
            at = xx * 1024 + kz * 128
            for arr, val in enumerate((grad_k, grad_v)):
                dst = slice(at + arr * 64, at + arr * 64 + 64)
                half0 = val[xx * 128 : xx * 128 + 64]
                half1 = val[xx * 128 + 64 : xx * 128 + 128]
                keep[dst] = jnp.where(core == 0, half0, half1)
                csend[dst] = jnp.where(core == 0, half1, half0).astype(BF16)
    grad_q = jnp.transpose(grad_qt) * scale
    gain_q = jnp.sum(grad_q * q_all[...].astype(F32), axis=0, keepdims=True)
    gains = jnp.concatenate([gain_q, gain_k, jnp.zeros((6, 128), F32)], 0)
    gkeep[...] = gains
    high = gains.astype(BF16).astype(F32)
    csend[4096:4112] = jnp.concatenate([high, gains - high], 0).astype(BF16)
    for z in range(NZ):
        osend[z, 0:64] = out_b[z * 64 : z * 64 + 64]
        osend[z, 64:128] = grad_q[z * 64 : z * 64 + 64].astype(BF16)


def gains_of(rows16):
    wide = rows16.astype(F32)
    return wide[0:8] + wide[8:16]


def core_sum_kernel(idx, keep, gkeep, other, after, s0, g0, s1, s2, s3):
    my_x = idx[0]
    gains = gkeep[...] + gains_of(other[4096:4112])
    g0[...] = gains
    high = gains.astype(BF16).astype(F32)
    rows = jnp.concatenate([high, gains - high], 0).astype(BF16)
    for d, ref in enumerate((s0, s1, s2, s3)):
        at = pl.multiple_of(lax.rem(my_x + d, NX) * 1024, 1024)
        total = keep[pl.ds(at, 1024)] + other[pl.ds(at, 1024)].astype(F32)
        ref[0:1024] = total.astype(ref.dtype)
        if d:
            ref[1024:1040] = rows


def ring_sum_kernel(s0, g0, r1, r2, r3, osend, after, out, done):
    done[...] = g0[...]
    gains = g0[...] + gains_of(r1[1024:1040]) + gains_of(r2[1024:1040]) + gains_of(r3[1024:1040])
    high = gains.astype(BF16).astype(F32)
    rows = jnp.concatenate([high, gains - high], 0).astype(BF16)
    for z in range(NZ):
        at = slice(z * 128, z * 128 + 128)
        total = s0[at] + r1[at].astype(F32) + r2[at].astype(F32) + r3[at].astype(F32)
        out[z, 0:128] = total.astype(BF16)
        out[z, 128:256] = osend[z]
        out[z, 256:272] = rows


def inner_kernel(idx, back, mine, other, gn_q, gn_k, after, part, gains_q, gains_k):
    core = idx[1]
    sum_q = jnp.zeros((64, 128), F32)
    sum_k = jnp.zeros((64, 128), F32)
    for ref, gain, first in ((mine, own_gains(gn_q, gn_k), core * 4), (other, other_gains(other), (1 - core) * 4)):
        for h in range(4):
            cols = slice(h * 128, (h + 1) * 128)
            gk = back[first + h, 0:64].astype(F32)
            gq = back[first + h, 192:256].astype(F32)
            sum_q = sum_q + gq * gain[0:1, cols] * ref[128:192, cols].astype(F32)
            sum_k = sum_k + gk * gain[1:2, cols] * ref[0:64, cols].astype(F32)
    part[...] = to_lanes(
        jnp.sum(sum_q, axis=1, keepdims=True), jnp.sum(sum_k, axis=1, keepdims=True)
    )
    for h in range(4):
        cols = slice(h * 128, (h + 1) * 128)
        got = gains_of(back[core * 4 + h, 256:272])
        gains_q[0:1, cols] = got[0:1] / gn_q[:, cols]
        gains_k[0:1, cols] = got[1:2] / gn_k[:, cols]


def norm_kernel(idx, back, mine, other, gn_q, gn_k, rates, p0, p1, p2, p3, keep, send):
    core = idx[1]
    rate_q, rate_k = to_columns(rates[...])
    inner_q, inner_k = to_columns(p0[...] + p1[...] + p2[...] + p3[...])
    width = NY * 8 * HD
    coef_q = rate_q * rate_q * rate_q * inner_q / width
    coef_k = rate_k * rate_k * rate_k * inner_k / width
    for ref, gain, first, dst in (
        (mine, own_gains(gn_q, gn_k), core * 4, keep), (other, other_gains(other), (1 - core) * 4, send)
    ):
        for h in range(4):
            cols = slice(h * 128, (h + 1) * 128)
            gk = back[first + h, 0:64].astype(F32)
            gq = back[first + h, 192:256].astype(F32)
            raw_k, raw_q = ref[0:64, cols].astype(F32), ref[128:192, cols].astype(F32)
            dst[0, :, cols] = (rate_q * (gq * gain[0:1, cols]) - raw_q * coef_q).astype(BF16)
            dst[1, :, cols] = (rate_k * (gk * gain[1:2, cols]) - raw_k * coef_k).astype(BF16)
            dst[2, :, cols] = back[first + h, 64:128]
            dst[3, :, cols] = back[first + h, 128:192]


def join_kernel(idx, mine, got, q_out, k_out, v_out, o_out):
    core = idx[1]
    here = pl.ds(pl.multiple_of(core * HALF, HALF), HALF)
    there = pl.ds(pl.multiple_of((1 - core) * HALF, HALF), HALF)
    for slot, dst in enumerate((q_out, k_out, v_out, o_out)):
        dst[here, :] = mine[slot]
        dst[there, :] = got[slot]


def rotate(x, axis, size, by):
    return lax.ppermute(x, axis, [(i, (i + by) % size) for i in range(size)])


def flip(x, axis, size, by):
    return lax.ppermute(x, axis, [(i, i ^ by) for i in range(size)])


def along(x, by):
    count = NZ * NX
    return lax.ppermute(
        x, ("z", "x"), [(i, i + by) for i in range(count) if 0 <= i + by < count]
    )


def add16(a, b):
    return (a.astype(F32) + b.astype(F32)).astype(BF16)


def local(
    streams, short_filter, long_filter, hyena_grad, queries, keys, values, gain_q, gain_k, attn_grad
):
    channels = streams.shape[2]
    my_x = lax.axis_index("x")
    core = lax.axis_index("c")
    idx = jnp.stack([my_x, core, lax.axis_index("z")]).astype(jnp.int32)

    gains = (gain_q.reshape(1, 512), gain_k.reshape(1, 512))
    ANY = pl.BlockSpec(memory_space=pl.ANY)
    tab = jnp.asarray(transform_tables())
    st = streams.transpose(1, 0, 2)
    sf = short_filter.transpose(1, 0, 2)
    mine, send, to_next, to_prev, to_second = call(
        halves_kernel,
        [
            shape((256, 512), BF16), shape((272, 512), BF16), shape((272, channels), BF16),
            shape((256, channels), BF16), shape((32, channels), BF16),
        ],
        [pltpu.SemaphoreType.DMA((15,))],
        in_specs=[SM] + [ANY] * 6 + [VM] * 2,
        out_specs=[VM] * 5,
        us=1.0,
        vmem=60,
    )(idx, keys, values, queries, attn_grad, st, hyena_grad, *gains)
    other = rotate(send, "c", NC, 1)
    second = along(to_second, 2)
    prev = along(to_next, 1)
    following = along(to_prev, -1)

    squares = call(square_kernel, shape((8, 128), F32), in_specs=[VM, VM], out_specs=VM, us=0.7)(mine, other)
    sums = [squares] + [rotate(squares, "y", NY, d) for d in (1, 3, 2)]
    payload, rates = call(
        pack_kernel,
        [shape((8, 256, 128), BF16), shape((8, 128), F32)],
        in_specs=[SM] + [VM] * 8 + [ANY] * 3,
        out_specs=[VM, VM],
        us=1.5,
    )(idx, mine, other, *gains, *sums, prev, following, second)
    blk = lax.all_to_all(payload, "z", 0, 0)

    tile = 256
    grid = (channels // tile,)

    def spec(*lead):
        zeros = (0,) * len(lead)
        return pl.BlockSpec(lead + (tile,), lambda i: zeros + (i,))

    def whole(*dims):
        zeros = (0,) * len(dims)
        return pl.BlockSpec(dims, lambda i: zeros)

    hyena_out, gs, head, tail, red, hyena_done = call(
        hyena_kernel,
        [
            shape((ROWS, channels), BF16),
            shape((3, ROWS, channels), BF16),
            shape((3, 16, channels), BF16),
            shape((3, 16, channels), F32),
            shape((NX, NZ, 48, 128), BF16),
            shape((8, 128), F32),
        ],
        [pltpu.VMEM((3, 272, tile), F32), pltpu.VMEM((3, 144, tile), F32)],
        grid=grid,
        in_specs=[
            spec(3, 128), spec(272), spec(32), spec(256), spec(128),
            spec(3, 7), spec(128), whole(2, 1280, 128), ANY,
        ],
        out_specs=[
            spec(128), spec(3, 128), spec(3, 16), spec(3, 16), pl.BlockSpec((NX, 2, 48, 128), lambda i: (0, i, 0, 0)), VM,
        ],
        us=11.0, vmem=56,
    )(st, prev, second, following, hyena_grad, sf, long_filter, tab, rates)
    next_head = along(head, -1)

    kv = call(
        keys_kernel, shape((NZ * 128, HD), BF16), in_specs=[VM, ANY], out_specs=VM, us=0.5
    )(blk, hyena_done)
    piece_shape = shape((NZ, 48, 128), BF16)
    ring, *parts = call(
        stack_kernel,
        [shape((NX, NZ * 128, HD), BF16)] + [piece_shape] * NX,
        in_specs=[SM] + [VM] * 5, out_specs=[VM] * 5, us=1.0,
    )(idx, kv, *[rotate(kv, "x", NX, d) for d in (2, 1, 3)], red)
    parts = parts[:1] + [rotate(parts[d], "x", NX, d) for d in (1, 2, 3)]
    pair = rotate(ring, "c", NC, 1)

    keep, gkeep, csend, osend = call(
        attention_kernel,
        [
            shape((4096, 128), F32), shape((8, 128), F32), shape((4112, 128), BF16),
            shape((8, 128, 128), BF16),
        ],
        [
            pltpu.VMEM((8, 512, 128), BF16), pltpu.VMEM((8, 512, 128), BF16),
            pltpu.VMEM((512, 128), BF16), pltpu.VMEM((512, 128), BF16),
            pltpu.VMEM((8, 512, 512), F32), pltpu.VMEM((8, 512, 512), BF16),
        ],
        in_specs=[SM] + [VM] * 3,
        out_specs=[VM] * 4,
        us=7.0, vmem=28,
    )(idx, blk, ring, pair)
    from_core = rotate(csend, "c", NC, 1)

    token = shape((8, 128), F32)
    piece, scattered = call(
        scatter_sum_kernel, [piece_shape, token], in_specs=[VM] * 4 + [ANY], out_specs=[VM] * 2, us=0.6
    )(*parts, gkeep)
    s0, g0, s1, s2, s3 = call(
        core_sum_kernel,
        [shape((1024, 128), F32), shape((8, 128), F32)] + [shape((1040, 128), BF16)] * 3,
        in_specs=[SM] + [VM] * 3 + [ANY],
        out_specs=[VM] * 5,
        us=1.0,
    )(idx, keep, gkeep, from_core, scattered)
    rest = [rotate(s, "x", NX, d) for d, s in ((1, s1), (3, s3), (2, s2))]
    for by in (1, 4, 2):
        piece, added = call(
            pair_sum_kernel, [piece_shape, token], in_specs=[VM] * 2 + [ANY], out_specs=[VM] * 2, us=0.6
        )(piece, flip(piece, "z", NZ, by), g0)
    outgoing, summed = call(
        ring_sum_kernel,
        [shape((8, 272, 128), BF16), shape((8, 128), F32)],
        in_specs=[VM] * 6 + [ANY], out_specs=[VM] * 2, us=1.0,
    )(s0, g0, *rest, osend, added)
    back = lax.all_to_all(outgoing, "z", 0, 0)

    pieces = [piece] + [rotate(piece, "x", NX, d) for d in (1, 3, 2)]
    grad_long, short_rows, filters = call(
        filter_kernel,
        [shape((128, channels), F32), shape((3, 7, channels), F32), shape((8, 128), F32)],
        in_specs=[SM] + [VM] * 4, out_specs=[VM] * 3, scratch=[pltpu.VMEM((192, channels), F32)],
        us=1.0,
    )(idx, *pieces)
    grad_short = short_rows.transpose(1, 0, 2)
    half_shape = shape((4, HALF, 512), BF16)
    part, gain_grad_q, gain_grad_k = call(
        inner_kernel,
        [shape((8, 128), F32), shape((1, 512), F32), shape((1, 512), F32)],
        in_specs=[SM] + [VM] * 5 + [ANY],
        out_specs=[VM] * 3,
        us=1.0,
    )(idx, back, mine, other, *gains, filters)
    parts = [part] + [rotate(part, "y", NY, d) for d in (1, 3, 2)]
    kept, send = call(
        norm_kernel,
        [half_shape, half_shape],
        in_specs=[SM] + [VM] * 10,
        out_specs=[VM] * 2,
        us=1.0,
    )(idx, back, mine, other, *gains, rates, *parts)
    got = rotate(send, "c", NC, 1)
    grad_q, grad_k, grad_v, attn_out = call(
        join_kernel,
        [shape((ROWS, 512), BF16)] * 4,
        in_specs=[SM] + [VM] * 2,
        out_specs=[VM] * 4,
        us=1.0,
    )(idx, kept, got)

    after = next_head.astype(F32)
    extra = jnp.zeros((3, 16, channels), F32)
    for j in range(1, 7):
        moved = jnp.pad(after[:, 0:j], ((0, 0), (16 - j, 0), (0, 0)))
        extra = extra + sf[:, j : j + 1] * moved
    last = (tail + extra).astype(BF16)
    grad_streams = jnp.concatenate([gs[:, 0:112], last], 1).transpose(1, 0, 2)
    return (
        hyena_out, grad_streams, grad_short, grad_long, attn_out, grad_q, grad_k, grad_v,
        gain_grad_q.reshape(512), gain_grad_k.reshape(512),
    )


def solution(mesh):
    fine = Mesh(mesh.devices.reshape(NZ, NX, NY, NC), ("z", "x", "y", "c"))
    ctx, tp = ("z", "x"), ("y", "c")
    return jax.shard_map(
        local,
        mesh=fine,
        in_specs=(
            P(ctx, None, tp), P(None, None, tp), P(None, tp), P(ctx, tp), P(ctx, tp),
            P(ctx, tp), P(ctx, tp), P(tp), P(tp), P(ctx, tp),
        ),
        out_specs=(
            P(ctx, tp), P(ctx, None, tp), P(None, None, tp), P(None, tp), P(ctx, tp),
            P(ctx, tp), P(ctx, tp), P(ctx, tp), P(tp), P(tp),
        ),
        check_vma=False,
    )
```

```python
import functools
import math

import jax
import jax.numpy as jnp
import numpy as np
from jax import lax
from jax.experimental import pallas as pl
from jax.experimental.pallas import tpu as pltpu
from jax.sharding import Mesh
from jax.sharding import PartitionSpec as P

HD = 128
EPS = 1e-06
MASKED = -1e30
ROWS = 128
NZ, NX, NY, NC = 8, 4, 4, 2
HALF = 64
F32 = jnp.float32
BF16 = jnp.bfloat16
MIB = 1024 * 1024


def call(kernel, outs, scratch=(), us=1.0, vmem=6, **kw):
    return pl.pallas_call(
        kernel,
        out_shape=outs,
        scratch_shapes=list(scratch),
        compiler_params=pltpu.CompilerParams(vmem_limit_bytes=vmem * MIB),
        cost_estimate=pl.CostEstimate(flops=int(us * 1.1e9), bytes_accessed=0, transcendentals=0),
        **kw,
    )


def shape(dims, dtype):
    return jax.ShapeDtypeStruct(dims, dtype)


VM = pl.BlockSpec(memory_space=pltpu.VMEM)
SM = pl.BlockSpec(memory_space=pltpu.SMEM)


def transform_tables():
    n = np.arange(256)
    k = np.arange(128) + 0.5
    angle = 2.0 * np.pi * np.outer(k, n) / 256.0
    fwd = np.concatenate([np.cos(angle), -np.sin(angle)], 0)
    inv = np.concatenate([np.cos(angle), -np.sin(angle)], 0).T / 128.0
    lag = inv[128 - np.arange(128)]
    pieces = [fwd[:, :128], fwd[:, 128:]]
    for t in (inv[128:], inv[:128], lag):
        pieces += [t[:, :128], t[:, 128:]]
    t32 = np.concatenate(pieces, 0).astype(np.float32)
    hi = t32.astype(jnp.bfloat16)
    lo = (t32 - hi.astype(np.float32)).astype(jnp.bfloat16)
    return np.stack([hi, lo])


def mm(a, b):
    return jnp.dot(a, b, preferred_element_type=F32)


def table_dot(table, at, x):
    rows = 256 if at < 512 else 128
    hi, lo = table[0, at : at + rows], table[1, at : at + rows]
    if x.dtype == BF16:
        return mm(hi, x) + mm(lo, x)
    xh = x.astype(BF16)
    xl = (x - xh.astype(F32)).astype(BF16)
    return mm(hi, xh) + mm(lo, xh) + mm(hi, xl)


def hyena_kernel(
    st, prev, second, following, hg, sf, lf, tab, after,
    out, gs, head, tail, red, done, ext, gm,
):
    done[...] = jnp.zeros((8, 128), F32)
    def taps(s):
        total = None
        for j in range(7):
            term = sf[s, j : j + 1, :] * ext[s, 16 - j : 272 - j, :]
            total = term if total is None else total + term
        return total

    ext[0, 0:16] = prev[256:272].astype(F32)
    ext[0, 16:144] = st[0].astype(F32)
    ext[0, 144:272] = following[0:128].astype(F32)
    for s in (1, 2):
        ext[s, 0:16] = second[16 * s - 16 : 16 * s].astype(F32)
        ext[s, 16:144] = prev[128 * s - 128 : 128 * s].astype(F32)
        ext[s, 144:272] = st[s].astype(F32)
    gates, ones, twos = taps(0), taps(1), taps(2)
    gate, one, two = gates[0:128], ones[128:256], twos[128:256]
    prod = (ones * twos).astype(BF16)
    up = hg[...].astype(F32)
    gf = up * gate
    gf_next = (following[128:256].astype(F32) * gates[128:256]).astype(BF16)
    spec_x = table_dot(tab, 0, prod[0:128]) + table_dot(tab, 256, prod[128:256])
    spec_h = table_dot(tab, 0, lf[...])
    spec_g0 = table_dot(tab, 0, gf)
    spec_g = spec_g0 + table_dot(tab, 256, gf_next)
    xr, xi = spec_x[:128], spec_x[128:]
    hr, hi = spec_h[:128], spec_h[128:]
    filt = table_dot(tab, 512, xr * hr - xi * hi) + table_dot(tab, 640, xr * hi + xi * hr)
    out[...] = (gate * filt).astype(BF16)
    gr, gi = spec_g[:128], spec_g[128:]
    gprod = table_dot(tab, 768, gr * hr + gi * hi) + table_dot(tab, 896, gi * hr - gr * hi)
    ar, ai = spec_g0[:128], spec_g0[128:]
    glong = table_dot(tab, 1024, ar * xr + ai * xi) + table_dot(tab, 1152, ar * xi - ai * xr)
    gm[:, 128:144] = jnp.zeros_like(gm[:, 128:144])
    gm[0, 0:128] = up * filt
    gm[1, 0:128] = gprod * two
    gm[2, 0:128] = gprod * one
    rows = []
    for s in range(3):
        head[s] = gm[s, 0:16].astype(BF16)
        base = 144 if s else 16
        own = gm[s, 0:128]
        total = None
        for j in range(7):
            term = sf[s, j : j + 1, :] * gm[s, j : j + 128, :]
            total = term if total is None else total + term
            rows.append(jnp.sum(own * ext[s, base - j : base + 128 - j, :], axis=0, keepdims=True))
        rows.append(jnp.zeros_like(rows[-1]))
        gs[s] = total.astype(BF16)
        tail[s] = total[112:128]
    rows.append(jnp.zeros((40, rows[-1].shape[1]), F32))
    every = jnp.concatenate([glong] + rows, 0).astype(BF16)
    for part in range(8):
        at, col = (part % 4) * 48, (part // 4) * 128
        red[part % 4, part // 4] = every[at : at + 48, col : col + 128]


def filter_kernel(idx, p0, p1, p3, p2, long_out, short_out, done, every):
    done[...] = jnp.zeros((8, 128), F32)
    my_x = idx[0]
    for d, ref in ((0, p0), (1, p1), (2, p2), (3, p3)):
        at = pl.multiple_of(lax.rem(my_x + NX - d, NX) * 48, 48)
        for z in range(NZ):
            every[pl.ds(at, 48), z * 128 : z * 128 + 128] = ref[z].astype(F32)
    long_out[...] = every[0:128]
    for s in range(3):
        short_out[s] = every[128 + 8 * s : 135 + 8 * s]


def to_lanes(col_q, col_k):
    both = jnp.concatenate([col_q, col_k], 0)
    return jnp.transpose(jnp.broadcast_to(both, (128, 128)))[0:8]


def to_columns(lanes):
    wide = jnp.transpose(jnp.broadcast_to(lanes[0:1], (128, 128)))
    return wide[0:64, 0:1], wide[64:128, 0:1]


def lane_sum(x):
    total = x[:, 0:128]
    for h in range(1, x.shape[1] // 128):
        total = total + x[:, h * 128 : (h + 1) * 128]
    return jnp.sum(total, axis=1, keepdims=True)


def split3(x):
    high = x.astype(BF16).astype(F32)
    mid = (x - high).astype(BF16).astype(F32)
    return high, mid, x - high - mid


def halves_kernel(idx, keys, values, queries, grads, streams, hg, gq, gk, mine, send, to_next, to_prev, to_second, own_sums, sems):
    core = idx[1]
    here = pl.multiple_of(core * HALF, HALF)
    there = pl.multiple_of((1 - core) * HALF, HALF)
    end = pl.ds(ROWS - 16, 16)
    pairs = [
        (streams.at[1], to_next.at[pl.ds(0, ROWS)]),
        (streams.at[2], to_next.at[pl.ds(ROWS, ROWS)]),
        (streams.at[0, end], to_next.at[pl.ds(2 * ROWS, 16)]),
        (streams.at[0], to_prev.at[pl.ds(0, ROWS)]),
        (hg, to_prev.at[pl.ds(ROWS, ROWS)]),
        (streams.at[1, end], to_second.at[pl.ds(0, 16)]),
        (streams.at[2, end], to_second.at[pl.ds(16, 16)]),
    ]
    for a, ref in enumerate((keys, values, queries, grads)):
        dst = pl.ds(a * HALF, HALF)
        pairs.append((ref.at[pl.ds(there, HALF)], send.at[dst]))
        pairs.append((ref.at[pl.ds(here, HALF)], mine.at[dst]))
    copies = [pltpu.make_async_copy(src, dst, sems.at[i]) for i, (src, dst) in enumerate(pairs)]
    for c in copies:
        c.start()
    both = jnp.concatenate([gq[...], gk[...]], 0)
    parts = list(split3(both)) + [jnp.zeros((10, 512), F32)]
    send[256:272] = jnp.concatenate(parts, 0).astype(BF16)
    for c in copies:
        c.wait()
    own_sums[...] = squares_of(mine)


def own_gains(gn_q, gn_k):
    return jnp.concatenate([gn_q[...], gn_k[...]], 0)


def other_gains(other):
    wide = other[256:272].astype(F32)
    return wide[0:2] + wide[2:4] + wide[4:6]


def squares_of(rows):
    sums = []
    for slot in (2, 0):
        wide = rows[slot * HALF : slot * HALF + HALF].astype(F32)
        sums.append(lane_sum(wide * wide))
    return to_lanes(sums[0], sums[1])


def square_kernel(own_sums, other, out):
    out[...] = own_sums[...] + squares_of(other)


def pack_kernel(idx, mine, other, gn_q, gn_k, s0, s1, s2, s3, h0, h1, h2, out, rates, done):
    done[...] = jnp.zeros((8, 128), F32)
    core = idx[1]
    rate = lax.rsqrt((s0[...] + s1[...] + s2[...] + s3[...]) / (NY * 8 * HD) + EPS)
    rates[...] = rate
    rate_q, rate_k = to_columns(rate)
    for ref, gains, first in ((mine, own_gains(gn_q, gn_k), core * 4), (other, other_gains(other), (1 - core) * 4)):
        for h in range(4):
            cols = slice(h * 128, (h + 1) * 128)
            key, query = ref[0:64, cols].astype(F32), ref[128:192, cols].astype(F32)
            out[first + h, 0:64] = (key * rate_k * gains[1:2, cols]).astype(BF16)
            out[first + h, 64:128] = ref[64:128, cols]
            out[first + h, 128:192] = (query * rate_q * gains[0:1, cols]).astype(BF16)
            out[first + h, 192:256] = ref[192:256, cols]


def keys_kernel(blk, after, out):
    for z in range(NZ):
        out[z * 128 : z * 128 + 128] = blk[z, 0:128]


def stack_kernel(idx, a, c, b, d, red, out, *parts):
    for i, ref in enumerate((a, b, c, d)):
        out[i] = ref[...]
    for d, part in enumerate(parts):
        part[...] = red[lax.rem(idx[0] + d, NX)]


def scatter_sum_kernel(p0, p1, p2, p3, after, out, done):
    done[...] = jnp.zeros((8, 128), F32)
    total = p0[...].astype(F32) + p1[...].astype(F32) + p2[...].astype(F32) + p3[...].astype(F32)
    out[...] = total.astype(BF16)


def pair_sum_kernel(a, b, after, out, done):
    done[...] = jnp.zeros((8, 128), F32)
    out[...] = (a[...].astype(F32) + b[...].astype(F32)).astype(BF16)


def attention_kernel(
    idx, blk, mine, pair,
    keep, gkeep, csend, osend,
    k_all, v_all, q_all, d_all, s_all, w_all,
):
    my_x, core = idx[0], idx[1]
    for d in range(NX):
        xd = lax.rem(my_x + NX - d, NX)
        for ref, cc in ((mine, core), (pair, 1 - core)):
            at = pl.multiple_of(xd * 128 + cc * 64, 64)
            for z in range(NZ):
                k_all[z, pl.ds(at, 64)] = ref[d, z * 128 : z * 128 + 64]
                v_all[z, pl.ds(at, 64)] = ref[d, z * 128 + 64 : z * 128 + 128]
    for z in range(NZ):
        q_all[z * 64 : z * 64 + 64] = blk[z, 128:192]
        d_all[z * 64 : z * 64 + 64] = blk[z, 192:256]
    scale = 1.0 / math.sqrt(HD)
    power = scale * math.log2(math.e)
    base = my_x * 128 + core * 64
    nt = (((1,), (1,)), ((), ()))
    tn = (((0,), (0,)), ((), ()))

    def first(kz):
        return (kz // 2) * 128

    key_row = lax.broadcasted_iota(jnp.int32, (512, 128), 0)
    lane = lax.broadcasted_iota(jnp.int32, (512, 128), 1)
    query_row = (lane // 64) * 512 + base + lane % 64

    row_max = jnp.full((1, 512), MASKED, F32)
    for kz in range(NZ):
        lo = first(kz)
        sc = lax.dot_general(k_all[kz], q_all[lo:512], nt, preferred_element_type=F32)
        diag = jnp.where(key_row + (kz % 2) * 512 <= query_row, sc[:, 0:128], MASKED)
        sc = diag if lo == 384 else jnp.concatenate([diag, sc[:, 128:]], 1)
        s_all[kz, :, lo:512] = sc
        top = jnp.max(sc, axis=0, keepdims=True)
        top = jnp.maximum(row_max[:, lo:], top)
        row_max = top if lo == 0 else jnp.concatenate([row_max[:, :lo], top], 1)
    row_sum = jnp.zeros((1, 512), F32)
    for kz in range(NZ):
        lo = first(kz)
        p = jnp.exp2((s_all[kz, :, lo:512] - row_max[:, lo:]) * power)
        s_all[kz, :, lo:512] = p
        more = row_sum[:, lo:] + jnp.sum(p, axis=0, keepdims=True)
        row_sum = more if lo == 0 else jnp.concatenate([row_sum[:, :lo], more], 1)
    inv = 1.0 / row_sum
    out_t = jnp.zeros((128, 512), F32)
    for kz in range(NZ):
        lo = first(kz)
        w = (s_all[kz, :, lo:512] * inv[:, lo:]).astype(BF16)
        w_all[kz, :, lo:512] = w
        piece = out_t[:, lo:] + lax.dot_general(v_all[kz], w, tn, preferred_element_type=F32)
        out_t = piece if lo == 0 else jnp.concatenate([out_t[:, :lo], piece], 1)
    out_b = jnp.transpose(out_t).astype(BF16)
    spread_col = jnp.sum(out_b.astype(F32) * d_all[...].astype(F32), axis=1, keepdims=True)
    spread = jnp.transpose(jnp.broadcast_to(spread_col, (512, 128)))[0:1]
    grad_qt = jnp.zeros((128, 512), F32)
    gain_k = jnp.zeros((1, 128), F32)
    for kz in range(NZ):
        lo = first(kz)
        w = w_all[kz, :, lo:512]
        dp = lax.dot_general(v_all[kz], d_all[lo:512], nt, preferred_element_type=F32)
        ds = (w.astype(F32) * (dp - spread[:, lo:])).astype(BF16)
        grad_v = mm(w, d_all[lo:512])
        grad_k = mm(ds, q_all[lo:512]) * scale
        piece = grad_qt[:, lo:] + lax.dot_general(k_all[kz], ds, tn, preferred_element_type=F32)
        grad_qt = piece if lo == 0 else jnp.concatenate([grad_qt[:, :lo], piece], 1)
        gain_k = gain_k + jnp.sum(grad_k * k_all[kz].astype(F32), axis=0, keepdims=True)
        for xx in range(NX):
            at = xx * 1024 + kz * 128
            for arr, val in enumerate((grad_k, grad_v)):
                dst = slice(at + arr * 64, at + arr * 64 + 64)
                half0 = val[xx * 128 : xx * 128 + 64]
                half1 = val[xx * 128 + 64 : xx * 128 + 128]
                keep[dst] = jnp.where(core == 0, half0, half1)
                csend[dst] = jnp.where(core == 0, half1, half0).astype(BF16)
    grad_q = jnp.transpose(grad_qt) * scale
    gain_q = jnp.sum(grad_q * q_all[...].astype(F32), axis=0, keepdims=True)
    gains = jnp.concatenate([gain_q, gain_k, jnp.zeros((6, 128), F32)], 0)
    gkeep[...] = gains
    high = gains.astype(BF16).astype(F32)
    csend[4096:4112] = jnp.concatenate([high, gains - high], 0).astype(BF16)
    for z in range(NZ):
        osend[z, 0:64] = out_b[z * 64 : z * 64 + 64]
        osend[z, 64:128] = grad_q[z * 64 : z * 64 + 64].astype(BF16)


def gains_of(rows16):
    wide = rows16.astype(F32)
    return wide[0:8] + wide[8:16]


def core_sum_kernel(idx, keep, gkeep, other, after, s0, g0, s1, s2, s3):
    my_x = idx[0]
    gains = gkeep[...] + gains_of(other[4096:4112])
    g0[...] = gains
    high = gains.astype(BF16).astype(F32)
    rows = jnp.concatenate([high, gains - high], 0).astype(BF16)
    for d, ref in enumerate((s0, s1, s2, s3)):
        at = pl.multiple_of(lax.rem(my_x + d, NX) * 1024, 1024)
        total = keep[pl.ds(at, 1024)] + other[pl.ds(at, 1024)].astype(F32)
        ref[0:1024] = total.astype(ref.dtype)
        if d:
            ref[1024:1040] = rows


def ring_sum_kernel(s0, g0, r1, r2, r3, osend, after, out, done):
    done[...] = g0[...]
    gains = g0[...] + gains_of(r1[1024:1040]) + gains_of(r2[1024:1040]) + gains_of(r3[1024:1040])
    high = gains.astype(BF16).astype(F32)
    rows = jnp.concatenate([high, gains - high], 0).astype(BF16)
    for z in range(NZ):
        at = slice(z * 128, z * 128 + 128)
        total = s0[at] + r1[at].astype(F32) + r2[at].astype(F32) + r3[at].astype(F32)
        out[z, 0:128] = total.astype(BF16)
        out[z, 128:256] = osend[z]
        out[z, 256:272] = rows


def inner_kernel(idx, back, mine, other, gn_q, gn_k, after, part, gains_q, gains_k):
    core = idx[1]
    sum_q = jnp.zeros((64, 128), F32)
    sum_k = jnp.zeros((64, 128), F32)
    for ref, gain, first in ((mine, own_gains(gn_q, gn_k), core * 4), (other, other_gains(other), (1 - core) * 4)):
        for h in range(4):
            cols = slice(h * 128, (h + 1) * 128)
            gk = back[first + h, 0:64].astype(F32)
            gq = back[first + h, 192:256].astype(F32)
            sum_q = sum_q + gq * gain[0:1, cols] * ref[128:192, cols].astype(F32)
            sum_k = sum_k + gk * gain[1:2, cols] * ref[0:64, cols].astype(F32)
    part[...] = to_lanes(
        jnp.sum(sum_q, axis=1, keepdims=True), jnp.sum(sum_k, axis=1, keepdims=True)
    )
    for h in range(4):
        cols = slice(h * 128, (h + 1) * 128)
        got = gains_of(back[core * 4 + h, 256:272])
        gains_q[0:1, cols] = got[0:1] / gn_q[:, cols]
        gains_k[0:1, cols] = got[1:2] / gn_k[:, cols]


def norm_kernel(idx, back, mine, other, gn_q, gn_k, rates, p0, p1, p2, p3, keep, send):
    core = idx[1]
    rate_q, rate_k = to_columns(rates[...])
    inner_q, inner_k = to_columns(p0[...] + p1[...] + p2[...] + p3[...])
    width = NY * 8 * HD
    coef_q = rate_q * rate_q * rate_q * inner_q / width
    coef_k = rate_k * rate_k * rate_k * inner_k / width
    for ref, gain, first, dst in (
        (mine, own_gains(gn_q, gn_k), core * 4, keep), (other, other_gains(other), (1 - core) * 4, send)
    ):
        for h in range(4):
            cols = slice(h * 128, (h + 1) * 128)
            gk = back[first + h, 0:64].astype(F32)
            gq = back[first + h, 192:256].astype(F32)
            raw_k, raw_q = ref[0:64, cols].astype(F32), ref[128:192, cols].astype(F32)
            dst[0, :, cols] = (rate_q * (gq * gain[0:1, cols]) - raw_q * coef_q).astype(BF16)
            dst[1, :, cols] = (rate_k * (gk * gain[1:2, cols]) - raw_k * coef_k).astype(BF16)
            dst[2, :, cols] = back[first + h, 64:128]
            dst[3, :, cols] = back[first + h, 128:192]


def join_kernel(idx, mine, got, q_out, k_out, v_out, o_out):
    core = idx[1]
    here = pl.ds(pl.multiple_of(core * HALF, HALF), HALF)
    there = pl.ds(pl.multiple_of((1 - core) * HALF, HALF), HALF)
    for slot, dst in enumerate((q_out, k_out, v_out, o_out)):
        dst[here, :] = mine[slot]
        dst[there, :] = got[slot]


def rotate(x, axis, size, by):
    return lax.ppermute(x, axis, [(i, (i + by) % size) for i in range(size)])


def flip(x, axis, size, by):
    return lax.ppermute(x, axis, [(i, i ^ by) for i in range(size)])


def along(x, by):
    count = NZ * NX
    return lax.ppermute(
        x, ("z", "x"), [(i, i + by) for i in range(count) if 0 <= i + by < count]
    )


def add16(a, b):
    return (a.astype(F32) + b.astype(F32)).astype(BF16)


def local(
    streams, short_filter, long_filter, hyena_grad, queries, keys, values, gain_q, gain_k, attn_grad
):
    channels = streams.shape[2]
    my_x = lax.axis_index("x")
    core = lax.axis_index("c")
    idx = jnp.stack([my_x, core, lax.axis_index("z")]).astype(jnp.int32)

    gains = (gain_q.reshape(1, 512), gain_k.reshape(1, 512))
    ANY = pl.BlockSpec(memory_space=pl.ANY)
    tab = jnp.asarray(transform_tables())
    st = streams.transpose(1, 0, 2)
    sf = short_filter.transpose(1, 0, 2)
    mine, send, to_next, to_prev, to_second, own_sums = call(
        halves_kernel,
        [
            shape((256, 512), BF16), shape((272, 512), BF16), shape((272, channels), BF16),
            shape((256, channels), BF16), shape((32, channels), BF16), shape((8, 128), F32),
        ],
        [pltpu.SemaphoreType.DMA((15,))],
        in_specs=[SM] + [ANY] * 6 + [VM] * 2,
        out_specs=[VM] * 6,
        us=1.0,
        vmem=60,
    )(idx, keys, values, queries, attn_grad, st, hyena_grad, *gains)
    other = rotate(send, "c", NC, 1)
    second = along(to_second, 2)
    prev = along(to_next, 1)
    following = along(to_prev, -1)

    squares = call(square_kernel, shape((8, 128), F32), in_specs=[VM, VM], out_specs=VM, us=0.7)(own_sums, other)
    sums = [squares] + [rotate(squares, "y", NY, d) for d in (1, 3, 2)]
    payload, rates, packed = call(
        pack_kernel,
        [shape((8, 256, 128), BF16), shape((8, 128), F32), shape((8, 128), F32)],
        in_specs=[SM] + [VM] * 8 + [ANY] * 3,
        out_specs=[VM] * 3,
        us=1.5,
    )(idx, mine, other, *gains, *sums, prev, following, second)
    blk = lax.all_to_all(payload, "z", 0, 0)

    tile = 256
    grid = (channels // tile,)

    def spec(*lead):
        zeros = (0,) * len(lead)
        return pl.BlockSpec(lead + (tile,), lambda i: zeros + (i,))

    def whole(*dims):
        zeros = (0,) * len(dims)
        return pl.BlockSpec(dims, lambda i: zeros)

    hyena_out, gs, head, tail, red, hyena_done = call(
        hyena_kernel,
        [
            shape((ROWS, channels), BF16),
            shape((3, ROWS, channels), BF16),
            shape((3, 16, channels), BF16),
            shape((3, 16, channels), F32),
            shape((NX, NZ, 48, 128), BF16),
            shape((8, 128), F32),
        ],
        [pltpu.VMEM((3, 272, tile), F32), pltpu.VMEM((3, 144, tile), F32)],
        grid=grid,
        in_specs=[
            spec(3, 128), spec(272), spec(32), spec(256), spec(128),
            spec(3, 7), spec(128), whole(2, 1280, 128), ANY,
        ],
        out_specs=[
            spec(128), spec(3, 128), spec(3, 16), spec(3, 16), pl.BlockSpec((NX, 2, 48, 128), lambda i: (0, i, 0, 0)), VM,
        ],
        us=11.0, vmem=56,
    )(st, prev, second, following, hyena_grad, sf, long_filter, tab, packed)
    next_head = along(head, -1)

    kv = call(
        keys_kernel, shape((NZ * 128, HD), BF16), in_specs=[VM, ANY], out_specs=VM, us=0.5
    )(blk, hyena_done)
    piece_shape = shape((NZ, 48, 128), BF16)
    ring, *parts = call(
        stack_kernel,
        [shape((NX, NZ * 128, HD), BF16)] + [piece_shape] * NX,
        in_specs=[SM] + [VM] * 5, out_specs=[VM] * 5, us=1.0,
    )(idx, kv, *[rotate(kv, "x", NX, d) for d in (2, 1, 3)], red)
    parts = parts[:1] + [rotate(parts[d], "x", NX, d) for d in (1, 2, 3)]
    pair = rotate(ring, "c", NC, 1)

    keep, gkeep, csend, osend = call(
        attention_kernel,
        [
            shape((4096, 128), F32), shape((8, 128), F32), shape((4112, 128), BF16),
            shape((8, 128, 128), BF16),
        ],
        [
            pltpu.VMEM((8, 512, 128), BF16), pltpu.VMEM((8, 512, 128), BF16),
            pltpu.VMEM((512, 128), BF16), pltpu.VMEM((512, 128), BF16),
            pltpu.VMEM((8, 512, 512), F32), pltpu.VMEM((8, 512, 512), BF16),
        ],
        in_specs=[SM] + [VM] * 3,
        out_specs=[VM] * 4,
        us=7.0, vmem=28,
    )(idx, blk, ring, pair)
    from_core = rotate(csend, "c", NC, 1)

    token = shape((8, 128), F32)
    piece, scattered = call(
        scatter_sum_kernel, [piece_shape, token], in_specs=[VM] * 4 + [ANY], out_specs=[VM] * 2, us=0.6
    )(*parts, gkeep)
    s0, g0, s1, s2, s3 = call(
        core_sum_kernel,
        [shape((1024, 128), F32), shape((8, 128), F32)] + [shape((1040, 128), BF16)] * 3,
        in_specs=[SM] + [VM] * 3 + [ANY],
        out_specs=[VM] * 5,
        us=1.0,
    )(idx, keep, gkeep, from_core, scattered)
    rest = [rotate(s, "x", NX, d) for d, s in ((1, s1), (3, s3), (2, s2))]
    for by in (1, 2, 4):
        piece, added = call(
            pair_sum_kernel, [piece_shape, token], in_specs=[VM] * 2 + [ANY], out_specs=[VM] * 2, us=0.6
        )(piece, flip(piece, "z", NZ, by), g0)
    outgoing, summed = call(
        ring_sum_kernel,
        [shape((8, 272, 128), BF16), shape((8, 128), F32)],
        in_specs=[VM] * 6 + [ANY], out_specs=[VM] * 2, us=1.0,
    )(s0, g0, *rest, osend, added)
    back = lax.all_to_all(outgoing, "z", 0, 0)

    pieces = [piece] + [rotate(piece, "x", NX, d) for d in (1, 3, 2)]
    grad_long, short_rows, filters = call(
        filter_kernel,
        [shape((128, channels), F32), shape((3, 7, channels), F32), shape((8, 128), F32)],
        in_specs=[SM] + [VM] * 4, out_specs=[VM] * 3, scratch=[pltpu.VMEM((192, channels), F32)],
        us=1.0,
    )(idx, *pieces)
    grad_short = short_rows.transpose(1, 0, 2)
    half_shape = shape((4, HALF, 512), BF16)
    part, gain_grad_q, gain_grad_k = call(
        inner_kernel,
        [shape((8, 128), F32), shape((1, 512), F32), shape((1, 512), F32)],
        in_specs=[SM] + [VM] * 5 + [ANY],
        out_specs=[VM] * 3,
        us=1.0,
    )(idx, back, mine, other, *gains, filters)
    parts = [part] + [rotate(part, "y", NY, d) for d in (1, 3, 2)]
    kept, send = call(
        norm_kernel,
        [half_shape, half_shape],
        in_specs=[SM] + [VM] * 10,
        out_specs=[VM] * 2,
        us=1.0,
    )(idx, back, mine, other, *gains, rates, *parts)
    got = rotate(send, "c", NC, 1)
    grad_q, grad_k, grad_v, attn_out = call(
        join_kernel,
        [shape((ROWS, 512), BF16)] * 4,
        in_specs=[SM] + [VM] * 2,
        out_specs=[VM] * 4,
        us=1.0,
    )(idx, kept, got)

    after = next_head.astype(F32)
    extra = jnp.zeros((3, 16, channels), F32)
    for j in range(1, 7):
        moved = jnp.pad(after[:, 0:j], ((0, 0), (16 - j, 0), (0, 0)))
        extra = extra + sf[:, j : j + 1] * moved
    last = (tail + extra).astype(BF16)
    grad_streams = jnp.concatenate([gs[:, 0:112], last], 1).transpose(1, 0, 2)
    return (
        hyena_out, grad_streams, grad_short, grad_long, attn_out, grad_q, grad_k, grad_v,
        gain_grad_q.reshape(512), gain_grad_k.reshape(512),
    )


def solution(mesh):
    fine = Mesh(mesh.devices.reshape(NZ, NX, NY, NC), ("z", "x", "y", "c"))
    ctx, tp = ("z", "x"), ("y", "c")
    return jax.shard_map(
        local,
        mesh=fine,
        in_specs=(
            P(ctx, None, tp), P(None, None, tp), P(None, tp), P(ctx, tp), P(ctx, tp),
            P(ctx, tp), P(ctx, tp), P(tp), P(tp), P(ctx, tp),
        ),
        out_specs=(
            P(ctx, tp), P(ctx, None, tp), P(None, None, tp), P(None, tp), P(ctx, tp),
            P(ctx, tp), P(ctx, tp), P(ctx, tp), P(tp), P(tp),
        ),
        check_vma=False,
    )
```

```python
import functools
import math

import jax
import jax.numpy as jnp
import numpy as np
from jax import lax
from jax.experimental import pallas as pl
from jax.experimental.pallas import tpu as pltpu
from jax.sharding import Mesh
from jax.sharding import PartitionSpec as P

HD = 128
EPS = 1e-06
MASKED = -1e30
ROWS = 128
NZ, NX, NY, NC = 8, 4, 4, 2
HALF = 64
F32 = jnp.float32
BF16 = jnp.bfloat16
MIB = 1024 * 1024


def call(kernel, outs, scratch=(), us=1.0, vmem=6, **kw):
    return pl.pallas_call(
        kernel,
        out_shape=outs,
        scratch_shapes=list(scratch),
        compiler_params=pltpu.CompilerParams(vmem_limit_bytes=vmem * MIB),
        cost_estimate=pl.CostEstimate(flops=int(us * 1.1e9), bytes_accessed=0, transcendentals=0),
        **kw,
    )


def shape(dims, dtype):
    return jax.ShapeDtypeStruct(dims, dtype)


VM = pl.BlockSpec(memory_space=pltpu.VMEM)
SM = pl.BlockSpec(memory_space=pltpu.SMEM)


def transform_tables():
    n = np.arange(256)
    k = np.arange(128) + 0.5
    angle = 2.0 * np.pi * np.outer(k, n) / 256.0
    fwd = np.concatenate([np.cos(angle), -np.sin(angle)], 0)
    inv = np.concatenate([np.cos(angle), -np.sin(angle)], 0).T / 128.0
    lag = inv[128 - np.arange(128)]
    pieces = [fwd[:, :128], fwd[:, 128:]]
    for t in (inv[128:], inv[:128], lag):
        pieces += [t[:, :128], t[:, 128:]]
    t32 = np.concatenate(pieces, 0).astype(np.float32)
    hi = t32.astype(jnp.bfloat16)
    lo = (t32 - hi.astype(np.float32)).astype(jnp.bfloat16)
    return np.stack([hi, lo])


def mm(a, b):
    return jnp.dot(a, b, preferred_element_type=F32)


def table_dot(table, at, x):
    rows = 256 if at < 512 else 128
    hi, lo = table[0, at : at + rows], table[1, at : at + rows]
    if x.dtype == BF16:
        return mm(hi, x) + mm(lo, x)
    xh = x.astype(BF16)
    xl = (x - xh.astype(F32)).astype(BF16)
    return mm(hi, xh) + mm(lo, xh) + mm(hi, xl)


def hyena_kernel(
    st, prev, second, following, hg, sf, lf, tab, after,
    out, gs, head, tail, red, done, ext, gm,
):
    done[...] = jnp.zeros((8, 128), F32)
    def taps(s):
        total = None
        for j in range(7):
            term = sf[s, j : j + 1, :] * ext[s, 16 - j : 272 - j, :]
            total = term if total is None else total + term
        return total

    ext[0, 0:16] = prev[256:272].astype(F32)
    ext[0, 16:144] = st[0].astype(F32)
    ext[0, 144:272] = following[0:128].astype(F32)
    for s in (1, 2):
        ext[s, 0:16] = second[16 * s - 16 : 16 * s].astype(F32)
        ext[s, 16:144] = prev[128 * s - 128 : 128 * s].astype(F32)
        ext[s, 144:272] = st[s].astype(F32)
    gates, ones, twos = taps(0), taps(1), taps(2)
    gate, one, two = gates[0:128], ones[128:256], twos[128:256]
    prod = (ones * twos).astype(BF16)
    up = hg[...].astype(F32)
    gf = up * gate
    gf_next = (following[128:256].astype(F32) * gates[128:256]).astype(BF16)
    spec_x = table_dot(tab, 0, prod[0:128]) + table_dot(tab, 256, prod[128:256])
    spec_h = table_dot(tab, 0, lf[...])
    spec_g0 = table_dot(tab, 0, gf)
    spec_g = spec_g0 + table_dot(tab, 256, gf_next)
    xr, xi = spec_x[:128], spec_x[128:]
    hr, hi = spec_h[:128], spec_h[128:]
    filt = table_dot(tab, 512, xr * hr - xi * hi) + table_dot(tab, 640, xr * hi + xi * hr)
    out[...] = (gate * filt).astype(BF16)
    gr, gi = spec_g[:128], spec_g[128:]
    gprod = table_dot(tab, 768, gr * hr + gi * hi) + table_dot(tab, 896, gi * hr - gr * hi)
    ar, ai = spec_g0[:128], spec_g0[128:]
    glong = table_dot(tab, 1024, ar * xr + ai * xi) + table_dot(tab, 1152, ar * xi - ai * xr)
    gm[:, 128:144] = jnp.zeros_like(gm[:, 128:144])
    gm[0, 0:128] = up * filt
    gm[1, 0:128] = gprod * two
    gm[2, 0:128] = gprod * one
    rows = []
    for s in range(3):
        head[s] = gm[s, 0:16].astype(BF16)
        base = 144 if s else 16
        own = gm[s, 0:128]
        total = None
        for j in range(7):
            term = sf[s, j : j + 1, :] * gm[s, j : j + 128, :]
            total = term if total is None else total + term
            rows.append(jnp.sum(own * ext[s, base - j : base + 128 - j, :], axis=0, keepdims=True))
        rows.append(jnp.zeros_like(rows[-1]))
        gs[s] = total.astype(BF16)
        tail[s] = total[112:128]
    rows.append(jnp.zeros((40, rows[-1].shape[1]), F32))
    every = jnp.concatenate([glong] + rows, 0).astype(BF16)
    for part in range(8):
        at, col = (part % 4) * 48, (part // 4) * 128
        red[part % 4, part // 4] = every[at : at + 48, col : col + 128]


def filter_kernel(idx, p0, p1, p3, p2, long_out, short_out, done, every):
    done[...] = jnp.zeros((8, 128), F32)
    my_x = idx[0]
    for d, ref in ((0, p0), (1, p1), (2, p2), (3, p3)):
        at = pl.multiple_of(lax.rem(my_x + NX - d, NX) * 48, 48)
        for z in range(NZ):
            every[pl.ds(at, 48), z * 128 : z * 128 + 128] = ref[z].astype(F32)
    long_out[...] = every[0:128]
    for s in range(3):
        short_out[s] = every[128 + 8 * s : 135 + 8 * s]


def to_lanes(col_q, col_k):
    both = jnp.concatenate([col_q, col_k], 0)
    return jnp.transpose(jnp.broadcast_to(both, (128, 128)))[0:8]


def to_columns(lanes):
    wide = jnp.transpose(jnp.broadcast_to(lanes[0:1], (128, 128)))
    return wide[0:64, 0:1], wide[64:128, 0:1]


def lane_sum(x):
    total = x[:, 0:128]
    for h in range(1, x.shape[1] // 128):
        total = total + x[:, h * 128 : (h + 1) * 128]
    return jnp.sum(total, axis=1, keepdims=True)


def split3(x):
    high = x.astype(BF16).astype(F32)
    mid = (x - high).astype(BF16).astype(F32)
    return high, mid, x - high - mid


def halves_kernel(idx, keys, values, queries, grads, streams, hg, gq, gk, mine, send, to_next, to_prev, to_second, own_sums, sems):
    core = idx[1]
    here = pl.multiple_of(core * HALF, HALF)
    there = pl.multiple_of((1 - core) * HALF, HALF)
    end = pl.ds(ROWS - 16, 16)
    pairs = [
        (streams.at[1], to_next.at[pl.ds(0, ROWS)]),
        (streams.at[2], to_next.at[pl.ds(ROWS, ROWS)]),
        (streams.at[0, end], to_next.at[pl.ds(2 * ROWS, 16)]),
        (streams.at[0], to_prev.at[pl.ds(0, ROWS)]),
        (hg, to_prev.at[pl.ds(ROWS, ROWS)]),
        (streams.at[1, end], to_second.at[pl.ds(0, 16)]),
        (streams.at[2, end], to_second.at[pl.ds(16, 16)]),
    ]
    for a, ref in enumerate((keys, values, queries, grads)):
        dst = pl.ds(a * HALF, HALF)
        pairs.append((ref.at[pl.ds(there, HALF)], send.at[dst]))
        pairs.append((ref.at[pl.ds(here, HALF)], mine.at[dst]))
    copies = [pltpu.make_async_copy(src, dst, sems.at[i]) for i, (src, dst) in enumerate(pairs)]
    for c in copies:
        c.start()
    both = jnp.concatenate([gq[...], gk[...]], 0)
    parts = list(split3(both)) + [jnp.zeros((10, 512), F32)]
    send[256:272] = jnp.concatenate(parts, 0).astype(BF16)
    for c in copies:
        c.wait()
    own_sums[...] = squares_of(mine)


def own_gains(gn_q, gn_k):
    return jnp.concatenate([gn_q[...], gn_k[...]], 0)


def other_gains(other):
    wide = other[256:272].astype(F32)
    return wide[0:2] + wide[2:4] + wide[4:6]


def squares_of(rows):
    sums = []
    for slot in (2, 0):
        wide = rows[slot * HALF : slot * HALF + HALF].astype(F32)
        sums.append(lane_sum(wide * wide))
    return to_lanes(sums[0], sums[1])


def square_kernel(own_sums, other, out):
    out[...] = own_sums[...] + squares_of(other)


def pack_kernel(idx, mine, other, gn_q, gn_k, s0, s1, s2, s3, h0, h1, h2, out, rates, done):
    done[...] = jnp.zeros((8, 128), F32)
    core = idx[1]
    rate = lax.rsqrt((s0[...] + s1[...] + s2[...] + s3[...]) / (NY * 8 * HD) + EPS)
    rates[...] = rate
    rate_q, rate_k = to_columns(rate)
    for ref, gains, first in ((mine, own_gains(gn_q, gn_k), core * 4), (other, other_gains(other), (1 - core) * 4)):
        for h in range(4):
            cols = slice(h * 128, (h + 1) * 128)
            key, query = ref[0:64, cols].astype(F32), ref[128:192, cols].astype(F32)
            out[first + h, 0:64] = (key * rate_k * gains[1:2, cols]).astype(BF16)
            out[first + h, 64:128] = ref[64:128, cols]
            out[first + h, 128:192] = (query * rate_q * gains[0:1, cols]).astype(BF16)
            out[first + h, 192:256] = ref[192:256, cols]


def keys_kernel(blk, after, out):
    for z in range(NZ):
        out[z * 128 : z * 128 + 128] = blk[z, 0:128]


def stack_kernel(idx, a, c, b, d, red, out, *parts):
    for i, ref in enumerate((a, b, c, d)):
        out[i] = ref[...]
    for d, part in enumerate(parts):
        part[...] = red[lax.rem(idx[0] + d, NX)]


def scatter_sum_kernel(p0, p1, p2, p3, after, out, done):
    done[...] = jnp.zeros((8, 128), F32)
    total = p0[...].astype(F32) + p1[...].astype(F32) + p2[...].astype(F32) + p3[...].astype(F32)
    out[...] = total.astype(BF16)


def pair_sum_kernel(a, b, after, out, done):
    done[...] = jnp.zeros((8, 128), F32)
    out[...] = (a[...].astype(F32) + b[...].astype(F32)).astype(BF16)


def attention_kernel(
    idx, blk, mine, pair,
    keep, gkeep, csend, osend,
    k_all, v_all, q_all, d_all, s_all, w_all,
):
    my_x, core = idx[0], idx[1]
    for d in range(NX):
        xd = lax.rem(my_x + NX - d, NX)
        for ref, cc in ((mine, core), (pair, 1 - core)):
            at = pl.multiple_of(xd * 128 + cc * 64, 64)
            for z in range(NZ):
                k_all[z, pl.ds(at, 64)] = ref[d, z * 128 : z * 128 + 64]
                v_all[z, pl.ds(at, 64)] = ref[d, z * 128 + 64 : z * 128 + 128]
    for z in range(NZ):
        q_all[z * 64 : z * 64 + 64] = blk[z, 128:192]
        d_all[z * 64 : z * 64 + 64] = blk[z, 192:256]
    scale = 1.0 / math.sqrt(HD)
    power = scale * math.log2(math.e)
    base = my_x * 128 + core * 64
    nt = (((1,), (1,)), ((), ()))
    tn = (((0,), (0,)), ((), ()))

    def first(kz):
        return (kz // 2) * 128

    key_row = lax.broadcasted_iota(jnp.int32, (512, 128), 0)
    lane = lax.broadcasted_iota(jnp.int32, (512, 128), 1)
    query_row = (lane // 64) * 512 + base + lane % 64

    row_max = jnp.full((1, 512), MASKED, F32)
    for kz in range(NZ):
        lo = first(kz)
        sc = lax.dot_general(k_all[kz], q_all[lo:512], nt, preferred_element_type=F32)
        diag = jnp.where(key_row + (kz % 2) * 512 <= query_row, sc[:, 0:128], MASKED)
        sc = diag if lo == 384 else jnp.concatenate([diag, sc[:, 128:]], 1)
        s_all[kz, :, lo:512] = sc
        top = jnp.max(sc, axis=0, keepdims=True)
        top = jnp.maximum(row_max[:, lo:], top)
        row_max = top if lo == 0 else jnp.concatenate([row_max[:, :lo], top], 1)
    row_sum = jnp.zeros((1, 512), F32)
    for kz in range(NZ):
        lo = first(kz)
        p = jnp.exp2((s_all[kz, :, lo:512] - row_max[:, lo:]) * power)
        s_all[kz, :, lo:512] = p
        more = row_sum[:, lo:] + jnp.sum(p, axis=0, keepdims=True)
        row_sum = more if lo == 0 else jnp.concatenate([row_sum[:, :lo], more], 1)
    inv = 1.0 / row_sum
    out_t = jnp.zeros((128, 512), F32)
    for kz in range(NZ):
        lo = first(kz)
        w = (s_all[kz, :, lo:512] * inv[:, lo:]).astype(BF16)
        w_all[kz, :, lo:512] = w
        piece = out_t[:, lo:] + lax.dot_general(v_all[kz], w, tn, preferred_element_type=F32)
        out_t = piece if lo == 0 else jnp.concatenate([out_t[:, :lo], piece], 1)
    out_b = jnp.transpose(out_t).astype(BF16)
    spread_col = jnp.sum(out_b.astype(F32) * d_all[...].astype(F32), axis=1, keepdims=True)
    spread = jnp.transpose(jnp.broadcast_to(spread_col, (512, 128)))[0:1]
    grad_qt = jnp.zeros((128, 512), F32)
    gain_k = jnp.zeros((1, 128), F32)
    for kz in range(NZ):
        lo = first(kz)
        w = w_all[kz, :, lo:512]
        dp = lax.dot_general(v_all[kz], d_all[lo:512], nt, preferred_element_type=F32)
        ds = (w.astype(F32) * (dp - spread[:, lo:])).astype(BF16)
        grad_v = mm(w, d_all[lo:512])
        grad_k = mm(ds, q_all[lo:512]) * scale
        piece = grad_qt[:, lo:] + lax.dot_general(k_all[kz], ds, tn, preferred_element_type=F32)
        grad_qt = piece if lo == 0 else jnp.concatenate([grad_qt[:, :lo], piece], 1)
        gain_k = gain_k + jnp.sum(grad_k * k_all[kz].astype(F32), axis=0, keepdims=True)
        for xx in range(NX):
            at = xx * 1024 + kz * 128
            for arr, val in enumerate((grad_k, grad_v)):
                dst = slice(at + arr * 64, at + arr * 64 + 64)
                half0 = val[xx * 128 : xx * 128 + 64]
                half1 = val[xx * 128 + 64 : xx * 128 + 128]
                keep[dst] = jnp.where(core == 0, half0, half1)
                csend[dst] = jnp.where(core == 0, half1, half0).astype(BF16)
    grad_q = jnp.transpose(grad_qt) * scale
    gain_q = jnp.sum(grad_q * q_all[...].astype(F32), axis=0, keepdims=True)
    gains = jnp.concatenate([gain_q, gain_k, jnp.zeros((6, 128), F32)], 0)
    gkeep[...] = gains
    high = gains.astype(BF16).astype(F32)
    csend[4096:4112] = jnp.concatenate([high, gains - high], 0).astype(BF16)
    for z in range(NZ):
        osend[z, 0:64] = out_b[z * 64 : z * 64 + 64]
        osend[z, 64:128] = grad_q[z * 64 : z * 64 + 64].astype(BF16)


def gains_of(rows16):
    wide = rows16.astype(F32)
    return wide[0:8] + wide[8:16]


def core_sum_kernel(idx, keep, gkeep, other, after, s0, g0, s1, s2, s3):
    my_x = idx[0]
    gains = gkeep[...] + gains_of(other[4096:4112])
    g0[...] = gains
    high = gains.astype(BF16).astype(F32)
    rows = jnp.concatenate([high, gains - high], 0).astype(BF16)
    for d, ref in enumerate((s0, s1, s2, s3)):
        at = pl.multiple_of(lax.rem(my_x + d, NX) * 1024, 1024)
        total = keep[pl.ds(at, 1024)] + other[pl.ds(at, 1024)].astype(F32)
        ref[0:1024] = total.astype(ref.dtype)
        if d:
            ref[1024:1040] = rows


def ring_sum_kernel(s0, g0, r1, r2, r3, osend, after, out, done):
    done[...] = g0[...]
    gains = g0[...] + gains_of(r1[1024:1040]) + gains_of(r2[1024:1040]) + gains_of(r3[1024:1040])
    high = gains.astype(BF16).astype(F32)
    rows = jnp.concatenate([high, gains - high], 0).astype(BF16)
    for z in range(NZ):
        at = slice(z * 128, z * 128 + 128)
        total = s0[at] + r1[at].astype(F32) + r2[at].astype(F32) + r3[at].astype(F32)
        out[z, 0:128] = total.astype(BF16)
        out[z, 128:256] = osend[z]
        out[z, 256:272] = rows


def inner_kernel(idx, back, mine, other, gn_q, gn_k, after, part, gains_q, gains_k):
    core = idx[1]
    sum_q = jnp.zeros((64, 128), F32)
    sum_k = jnp.zeros((64, 128), F32)
    for ref, gain, first in ((mine, own_gains(gn_q, gn_k), core * 4), (other, other_gains(other), (1 - core) * 4)):
        for h in range(4):
            cols = slice(h * 128, (h + 1) * 128)
            gk = back[first + h, 0:64].astype(F32)
            gq = back[first + h, 192:256].astype(F32)
            sum_q = sum_q + gq * gain[0:1, cols] * ref[128:192, cols].astype(F32)
            sum_k = sum_k + gk * gain[1:2, cols] * ref[0:64, cols].astype(F32)
    part[...] = to_lanes(
        jnp.sum(sum_q, axis=1, keepdims=True), jnp.sum(sum_k, axis=1, keepdims=True)
    )
    for h in range(4):
        cols = slice(h * 128, (h + 1) * 128)
        got = gains_of(back[core * 4 + h, 256:272])
        gains_q[0:1, cols] = got[0:1] / gn_q[:, cols]
        gains_k[0:1, cols] = got[1:2] / gn_k[:, cols]


def norm_kernel(idx, back, mine, other, gn_q, gn_k, rates, p0, p1, p2, p3, keep, send):
    core = idx[1]
    rate_q, rate_k = to_columns(rates[...])
    inner_q, inner_k = to_columns(p0[...] + p1[...] + p2[...] + p3[...])
    width = NY * 8 * HD
    coef_q = rate_q * rate_q * rate_q * inner_q / width
    coef_k = rate_k * rate_k * rate_k * inner_k / width
    for ref, gain, first, dst in (
        (mine, own_gains(gn_q, gn_k), core * 4, keep), (other, other_gains(other), (1 - core) * 4, send)
    ):
        for h in range(4):
            cols = slice(h * 128, (h + 1) * 128)
            gk = back[first + h, 0:64].astype(F32)
            gq = back[first + h, 192:256].astype(F32)
            raw_k, raw_q = ref[0:64, cols].astype(F32), ref[128:192, cols].astype(F32)
            dst[0, :, cols] = (rate_q * (gq * gain[0:1, cols]) - raw_q * coef_q).astype(BF16)
            dst[1, :, cols] = (rate_k * (gk * gain[1:2, cols]) - raw_k * coef_k).astype(BF16)
            dst[2, :, cols] = back[first + h, 64:128]
            dst[3, :, cols] = back[first + h, 128:192]


def join_kernel(idx, mine, got, q_out, k_out, v_out, o_out):
    core = idx[1]
    here = pl.ds(pl.multiple_of(core * HALF, HALF), HALF)
    there = pl.ds(pl.multiple_of((1 - core) * HALF, HALF), HALF)
    for slot, dst in enumerate((q_out, k_out, v_out, o_out)):
        dst[here, :] = mine[slot]
        dst[there, :] = got[slot]


def rotate(x, axis, size, by):
    return lax.ppermute(x, axis, [(i, (i + by) % size) for i in range(size)])


def flip(x, axis, size, by):
    return lax.ppermute(x, axis, [(i, i ^ by) for i in range(size)])


def along(x, by):
    count = NZ * NX
    return lax.ppermute(
        x, ("z", "x"), [(i, i + by) for i in range(count) if 0 <= i + by < count]
    )


def add16(a, b):
    return (a.astype(F32) + b.astype(F32)).astype(BF16)


def local(
    streams, short_filter, long_filter, hyena_grad, queries, keys, values, gain_q, gain_k, attn_grad
):
    channels = streams.shape[2]
    my_x = lax.axis_index("x")
    core = lax.axis_index("c")
    idx = jnp.stack([my_x, core, lax.axis_index("z")]).astype(jnp.int32)

    gains = (gain_q.reshape(1, 512), gain_k.reshape(1, 512))
    ANY = pl.BlockSpec(memory_space=pl.ANY)
    tab = jnp.asarray(transform_tables())
    st = streams.transpose(1, 0, 2)
    sf = short_filter.transpose(1, 0, 2)
    mine, send, to_next, to_prev, to_second, own_sums = call(
        halves_kernel,
        [
            shape((256, 512), BF16), shape((272, 512), BF16), shape((272, channels), BF16),
            shape((256, channels), BF16), shape((32, channels), BF16), shape((8, 128), F32),
        ],
        [pltpu.SemaphoreType.DMA((15,))],
        in_specs=[SM] + [ANY] * 6 + [VM] * 2,
        out_specs=[VM] * 6,
        us=1.0,
        vmem=60,
    )(idx, keys, values, queries, attn_grad, st, hyena_grad, *gains)
    other = rotate(send, "c", NC, 1)
    second = along(to_second, 2)
    prev = along(to_next, 1)
    following = along(to_prev, -1)

    squares = call(square_kernel, shape((8, 128), F32), in_specs=[VM, VM], out_specs=VM, us=0.7)(own_sums, other)
    sums = [squares] + [rotate(squares, "y", NY, d) for d in (1, 3, 2)]
    payload, rates, packed = call(
        pack_kernel,
        [shape((8, 256, 128), BF16), shape((8, 128), F32), shape((8, 128), F32)],
        in_specs=[SM] + [VM] * 8 + [ANY] * 3,
        out_specs=[VM] * 3,
        us=1.5,
    )(idx, mine, other, *gains, *sums, prev, following, second)
    blk = lax.all_to_all(payload, "z", 0, 0)

    tile = 256
    grid = (channels // tile,)

    def spec(*lead):
        zeros = (0,) * len(lead)
        return pl.BlockSpec(lead + (tile,), lambda i: zeros + (i,))

    def whole(*dims):
        zeros = (0,) * len(dims)
        return pl.BlockSpec(dims, lambda i: zeros)

    hyena_out, gs, head, tail, red, hyena_done = call(
        hyena_kernel,
        [
            shape((ROWS, channels), BF16),
            shape((3, ROWS, channels), BF16),
            shape((3, 16, channels), BF16),
            shape((3, 16, channels), F32),
            shape((NX, NZ, 48, 128), BF16),
            shape((8, 128), F32),
        ],
        [pltpu.VMEM((3, 272, tile), F32), pltpu.VMEM((3, 144, tile), F32)],
        grid=grid,
        in_specs=[
            spec(3, 128), spec(272), spec(32), spec(256), spec(128),
            spec(3, 7), spec(128), whole(2, 1280, 128), VM,
        ],
        out_specs=[
            spec(128), spec(3, 128), spec(3, 16), spec(3, 16), pl.BlockSpec((NX, 2, 48, 128), lambda i: (0, i, 0, 0)), VM,
        ],
        us=11.0, vmem=56,
    )(st, prev, second, following, hyena_grad, sf, long_filter, tab, packed)
    next_head = along(head, -1)

    kv = call(
        keys_kernel, shape((NZ * 128, HD), BF16), in_specs=[VM, VM], out_specs=VM, us=0.5
    )(blk, hyena_done)
    piece_shape = shape((NZ, 48, 128), BF16)
    ring, *parts = call(
        stack_kernel,
        [shape((NX, NZ * 128, HD), BF16)] + [piece_shape] * NX,
        in_specs=[SM] + [VM] * 5, out_specs=[VM] * 5, us=1.0,
    )(idx, kv, *[rotate(kv, "x", NX, d) for d in (2, 1, 3)], red)
    parts = parts[:1] + [rotate(parts[d], "x", NX, d) for d in (1, 2, 3)]
    pair = rotate(ring, "c", NC, 1)

    keep, gkeep, csend, osend = call(
        attention_kernel,
        [
            shape((4096, 128), F32), shape((8, 128), F32), shape((4112, 128), BF16),
            shape((8, 128, 128), BF16),
        ],
        [
            pltpu.VMEM((8, 512, 128), BF16), pltpu.VMEM((8, 512, 128), BF16),
            pltpu.VMEM((512, 128), BF16), pltpu.VMEM((512, 128), BF16),
            pltpu.VMEM((8, 512, 512), F32), pltpu.VMEM((8, 512, 512), BF16),
        ],
        in_specs=[SM] + [VM] * 3,
        out_specs=[VM] * 4,
        us=7.0, vmem=28,
    )(idx, blk, ring, pair)
    from_core = rotate(csend, "c", NC, 1)

    token = shape((8, 128), F32)
    piece, scattered = call(
        scatter_sum_kernel, [piece_shape, token], in_specs=[VM] * 4 + [ANY], out_specs=[VM] * 2, us=0.6
    )(*parts, gkeep)
    s0, g0, s1, s2, s3 = call(
        core_sum_kernel,
        [shape((1024, 128), F32), shape((8, 128), F32)] + [shape((1040, 128), BF16)] * 3,
        in_specs=[SM] + [VM] * 3 + [ANY],
        out_specs=[VM] * 5,
        us=1.0,
    )(idx, keep, gkeep, from_core, scattered)
    rest = [rotate(s, "x", NX, d) for d, s in ((1, s1), (3, s3), (2, s2))]
    for by in (1, 2, 4):
        piece, added = call(
            pair_sum_kernel, [piece_shape, token], in_specs=[VM] * 2 + [ANY], out_specs=[VM] * 2, us=0.6
        )(piece, flip(piece, "z", NZ, by), g0)
    outgoing, summed = call(
        ring_sum_kernel,
        [shape((8, 272, 128), BF16), shape((8, 128), F32)],
        in_specs=[VM] * 6 + [ANY], out_specs=[VM] * 2, us=1.0,
    )(s0, g0, *rest, osend, added)
    back = lax.all_to_all(outgoing, "z", 0, 0)

    pieces = [piece] + [rotate(piece, "x", NX, d) for d in (1, 3, 2)]
    grad_long, short_rows, filters = call(
        filter_kernel,
        [shape((128, channels), F32), shape((3, 7, channels), F32), shape((8, 128), F32)],
        in_specs=[SM] + [VM] * 4, out_specs=[VM] * 3, scratch=[pltpu.VMEM((192, channels), F32)],
        us=1.0,
    )(idx, *pieces)
    grad_short = short_rows.transpose(1, 0, 2)
    half_shape = shape((4, HALF, 512), BF16)
    part, gain_grad_q, gain_grad_k = call(
        inner_kernel,
        [shape((8, 128), F32), shape((1, 512), F32), shape((1, 512), F32)],
        in_specs=[SM] + [VM] * 5 + [ANY],
        out_specs=[VM] * 3,
        us=1.0,
    )(idx, back, mine, other, *gains, filters)
    parts = [part] + [rotate(part, "y", NY, d) for d in (1, 3, 2)]
    kept, send = call(
        norm_kernel,
        [half_shape, half_shape],
        in_specs=[SM] + [VM] * 10,
        out_specs=[VM] * 2,
        us=1.0,
    )(idx, back, mine, other, *gains, rates, *parts)
    got = rotate(send, "c", NC, 1)
    grad_q, grad_k, grad_v, attn_out = call(
        join_kernel,
        [shape((ROWS, 512), BF16)] * 4,
        in_specs=[SM] + [VM] * 2,
        out_specs=[VM] * 4,
        us=1.0,
    )(idx, kept, got)

    after = next_head.astype(F32)
    extra = jnp.zeros((3, 16, channels), F32)
    for j in range(1, 7):
        moved = jnp.pad(after[:, 0:j], ((0, 0), (16 - j, 0), (0, 0)))
        extra = extra + sf[:, j : j + 1] * moved
    last = (tail + extra).astype(BF16)
    grad_streams = jnp.concatenate([gs[:, 0:112], last], 1).transpose(1, 0, 2)
    return (
        hyena_out, grad_streams, grad_short, grad_long, attn_out, grad_q, grad_k, grad_v,
        gain_grad_q.reshape(512), gain_grad_k.reshape(512),
    )


def solution(mesh):
    fine = Mesh(mesh.devices.reshape(NZ, NX, NY, NC), ("z", "x", "y", "c"))
    ctx, tp = ("z", "x"), ("y", "c")
    return jax.shard_map(
        local,
        mesh=fine,
        in_specs=(
            P(ctx, None, tp), P(None, None, tp), P(None, tp), P(ctx, tp), P(ctx, tp),
            P(ctx, tp), P(ctx, tp), P(tp), P(tp), P(ctx, tp),
        ),
        out_specs=(
            P(ctx, tp), P(ctx, None, tp), P(None, None, tp), P(None, tp), P(ctx, tp),
            P(ctx, tp), P(ctx, tp), P(ctx, tp), P(tp), P(tp),
        ),
        check_vma=False,
    )
```
